128 devices in a mesh: dp: 16 (over y, x), tensor: 8 (over z, core).
Axes of the slice: x: 4, y: 4, z: 4, core: 2. Of those that a mesh axis runs over, the one named last changes fastest.
Arguments:
- hidden_input: bfloat16 [16384, 8192], P('dp'), may hold values from -6 to 6
- key_value_gradient: bfloat16 [2, 16384, 1024], P(None, 'dp', 'tensor'), may hold values from -6 to 6
- key_value_weight: bfloat16 [2, 8192, 1024], P(None, None, 'tensor'), may hold values from -0.0625 to 0.0625
- down_adapters: bfloat16 [128, 32, 8192], P(None, None, 'tensor'), may hold values from -0.0625 to 0.0625
- up_adapters: bfloat16 [128, 2, 16, 1024], P(None, None, None, 'tensor'), may hold values from -0.1875 to 0.1875
- adapter_inner_saved: bfloat16 [32, 16384], P(None, 'dp'), may hold values from -2 to 2
- block_owner_tenant: int32 [128], P('dp'), may hold values from 0 to 127
- live_block_counts: int32 [16], P('dp'), may hold values from 1 to 8, as said below
- tenant_position: int32 [128], replicated, may hold values from 0 to 127, each once
Outputs:
- hidden_gradient: bfloat16 [16384, 8192], P('dp', 'tensor')
- grad_a: float32 [128, 32, 8192], P('dp', None, 'tensor')
- grad_b: float32 [128, 2, 16, 1024], P('dp', None, None, 'tensor')
The draws below stay inside these ranges and needn't reach their ends.
Inputs may be any that keep to these rules, and one draw needn't show every extreme that they name: `live_block_counts`: some index of dp has all 8 block slots live.
All inputs are finite; a program needn't handle non-finite values.
Results may differ from the reference program's by a relative error of at most 0.022.
Values may be sent and summed in bfloat16 or wider, within the bound.
A program may use at most 192 MiB of HBM per device.

```python
import math
import jax
import jax.numpy as jnp
import numpy as np
from jax import lax

MODEL_WIDTH = 8192
KV = 1024
ADAPTER_RANK = 16
BLOCK_TOKENS = 128
BLK_DEV = 8
TOKEN_SLOTS = 16384
BLOCK_SLOTS = 128
TENANTS = 128
N_DP = 16
N_TENSOR = 8


def draw_live_block_counts(key, part):
    key_one = jax.random.fold_in(key, 11)
    key_two = jax.random.fold_in(key, 12)
    counts = jax.random.randint(key_one, (N_DP,), 1, BLK_DEV + 1, dtype=jnp.int32)
    chosen = jax.random.randint(key_two, (), 0, N_DP, dtype=jnp.int32)
    return jnp.where(jnp.arange(N_DP, dtype=jnp.int32) == chosen, BLK_DEV, counts).astype(jnp.int32)


def with_ends(drawn, rng, smallest, top_value):
    longest = drawn.shape.index(max(drawn.shape))
    spots = []
    for shift in (0, 1):
        where = [jax.random.randint(jax.random.fold_in(rng, axis), (), 0, length) for axis, length in enumerate(drawn.shape)]
        where[longest] = (where[longest] + shift) % drawn.shape[longest]
        spots.append(tuple(where))
    return drawn.at[spots[0]].set(smallest).at[spots[1]].set(top_value)


def level_of(key, shape, shards, low, high):
    gain = 1.0
    for dim, parts in shards:
        draws = jax.random.uniform(jax.random.fold_in(jax.random.fold_in(key, 6), dim), (parts,), jnp.float32, low / len(shards), high / len(shards))
        gain = gain * jnp.repeat(jnp.exp(draws), shape[dim] // parts).reshape((-1,) + (1,) * (len(shape) - 1 - dim))
    return gain


def cumulative_ranks(amount, skew):
    portions = [(1 << 20) // math.isqrt(rank ** skew) + 1 for rank in range(1, amount + 1)]
    deviation = 1 + sum(portions) // (1 << 30)
    return np.cumsum(np.array([max(1, weight // deviation) for weight in portions]))


def ranked_ids(stream_key, dims, count, slope):
    table = cumulative_ranks(count, slope)
    ticket = jax.random.randint(jax.random.fold_in(stream_key, 1), dims, 0, int(table[count - 1]))
    grade = jnp.searchsorted(jnp.asarray(table, jnp.int32), ticket, side="right")
    return jax.random.permutation(jax.random.fold_in(stream_key, 2), count)[grade].astype(jnp.int32)


def scatter_about(own_key, shape, scale, reach, shards=(), kind=jnp.bfloat16):
    drawn = scale * jax.random.normal(own_key, shape, jnp.float32)
    if shards:
        drawn = drawn * level_of(own_key, shape, shards, -0.22, 0.18)
    return jnp.clip(drawn, -reach, reach).astype(kind)


def setup_inputs(seed: int = 0) -> dict:
    key_list = jax.random.split(jax.random.key(seed), 10)
    return {
        "hidden_input": scatter_about(key_list[0], (TOKEN_SLOTS, MODEL_WIDTH), 1.0, 6.0, ((0, 16),)),
        "key_value_gradient": scatter_about(key_list[1], (2, TOKEN_SLOTS, KV), 1.0, 6.0, ((1, 16), (2, 8))),
        "key_value_weight": scatter_about(key_list[2], (2, MODEL_WIDTH, KV), MODEL_WIDTH ** -0.5, 0.0625, ((2, 8),)),
        "down_adapters": scatter_about(key_list[3], (TENANTS, 2 * ADAPTER_RANK, MODEL_WIDTH), MODEL_WIDTH ** -0.5, 0.0625, ((2, 8),)),
        "up_adapters": scatter_about(key_list[4], (TENANTS, 2, ADAPTER_RANK, KV), KV ** -0.5, 0.1875, ((3, 8),)),
        "adapter_inner_saved": scatter_about(key_list[5], (2 * ADAPTER_RANK, TOKEN_SLOTS), 0.3, 2.0, ((1, 16),)),
        "block_owner_tenant": with_ends(ranked_ids(key_list[6], (BLOCK_SLOTS,), TENANTS, 2), jax.random.fold_in(key_list[6], 3), 0, TENANTS - 1).astype(jnp.int32),
        "live_block_counts": draw_live_block_counts(jax.random.fold_in(key_list[9], 71), 0),
        "tenant_position": jax.random.permutation(key_list[8], TENANTS).astype(jnp.int32),
    }


def reference(hidden_input, key_value_gradient, key_value_weight, down_adapters, up_adapters, adapter_inner_saved, block_owner_tenant, live_block_counts, tenant_position):
    live_blk = (jnp.arange(BLK_DEV, dtype=jnp.int32)[None, :] < live_block_counts[:, None]).reshape(BLOCK_SLOTS)
    live_tok = jnp.repeat(live_blk, BLOCK_TOKENS)
    grad = key_value_gradient * live_tok.astype(jnp.bfloat16)[None, :, None]
    slot_blk = tenant_position[block_owner_tenant]
    b_sel = up_adapters[block_owner_tenant].astype(jnp.float32)
    g_blk = grad.reshape(2, BLOCK_SLOTS, BLOCK_TOKENS, KV).astype(jnp.float32)
    inner = jnp.einsum('cbij,bcrj->bicr', g_blk, b_sel).reshape(BLOCK_SLOTS, BLOCK_TOKENS, 2 * ADAPTER_RANK)
    inner_block = inner.astype(jnp.bfloat16).astype(jnp.float32)
    width = KV // N_TENSOR
    total_sum = jnp.zeros((TOKEN_SLOTS, MODEL_WIDTH), jnp.float32)
    for group in range(N_TENSOR):
        cols = slice(group * width, (group + 1) * width)
        part = jnp.einsum('cnj,cdj->nd', grad[:, :, cols].astype(jnp.float32), key_value_weight[:, :, cols].astype(jnp.float32))
        part = lax.optimization_barrier(part.astype(jnp.bfloat16))
        total_sum = total_sum + part.astype(jnp.float32)
    selected_down = down_adapters[block_owner_tenant].astype(jnp.float32)
    adapter_input_gradient = jnp.einsum('hxr,hrg->hxg', inner_block, selected_down).reshape(TOKEN_SLOTS, MODEL_WIDTH)
    hidden_gradient = (total_sum + 2.0 * adapter_input_gradient).astype(jnp.bfloat16)
    x_blk = hidden_input.reshape(BLOCK_SLOTS, BLOCK_TOKENS, MODEL_WIDTH).astype(jnp.float32)
    per_a = 2.0 * jnp.einsum('bic,bid->bcd', inner_block, x_blk)
    hidden_block = adapter_inner_saved.reshape(2, ADAPTER_RANK, BLOCK_SLOTS, BLOCK_TOKENS).astype(jnp.float32)
    per_b = 2.0 * jnp.einsum('crbi,cbij->bcrj', hidden_block, g_blk)
    grad_a = jax.ops.segment_sum(per_a, slot_blk, TENANTS)
    grad_b = jax.ops.segment_sum(per_b, slot_blk, TENANTS)
    return hidden_gradient, grad_a, grad_b
```

```python
import jax
import jax.numpy as jnp
from jax import lax
from jax.experimental import pallas as pl
from jax.experimental.pallas import tpu as pltpu
from jax.sharding import PartitionSpec as P

MESH = pl.DeviceIdType.MESH
BF = jnp.bfloat16
F32 = jnp.float32
NT = (((1,), (1,)), ((), ()))
N_REMOTE = 80
N_LOCAL = 12


def comm_kernel(
    x_hbm, kvg_hbm, w_hbm, down_hbm, up_hbm, inner_hbm, owner_ref, live_ref, tp_ref,
    hg_hbm, ga_hbm, gb_hbm,
    gf, wf, xv, downv, upv, innerv, kvgv,
    upart, urecv, uz, ubf, ubd, asel,
    meta_a, meta_b, ea, eb, aga, agb,
    snd_a, snd_b, r1_a, r1_b, r2_a, r2_b, own_a, own_b, dns_a, dns_b,
    hgv, gav, gbv,
    ss, rs, ls,
):
    dp = lax.axis_index("dp")
    t = lax.axis_index("tensor")
    y, x = dp // 4, dp % 4
    z, c = t // 2, t % 2

    def xdev(d):
        return (y * 4 + (x + d) % 4, t)

    def ydev(d):
        return (((y + d) % 4) * 4 + x, t)

    def zdev(d, rel):
        return (dp, ((z + d) % 4) * 2 + (c + rel) % 2)

    sib = zdev(0, 1)
    count = [0, 0]
    pending = []

    def rcopy(src, dst, dev):
        k = count[0]
        count[0] += 1
        cp = pltpu.make_async_remote_copy(
            src_ref=src, dst_ref=dst, send_sem=ss.at[k], recv_sem=rs.at[k],
            device_id=dev, device_id_type=MESH,
        )
        cp.start()
        pending.append(cp)
        return cp

    def lcopy(src, dst):
        k = count[1]
        count[1] += 1
        cp = pltpu.make_async_copy(src, dst, ls.at[k])
        cp.start()
        return cp

    peers = [sib]
    peers += [zdev(d, rel) for d in (1, 2, 3) for rel in (0, 1)]
    peers += [xdev(d) for d in (1, 2, 3)] + [ydev(d) for d in (1, 2, 3)]
    barrier = pltpu.get_barrier_semaphore()
    for dev in peers:
        pl.semaphore_signal(barrier, inc=1, device_id=dev, device_id_type=MESH)

    l_kvg = lcopy(kvg_hbm, kvgv)
    l_up = lcopy(up_hbm, upv)
    l_inner = lcopy(inner_hbm, innerv)
    l_w = lcopy(w_hbm.at[:, pl.ds(t * 1024, 1024), :], wf.at[0])
    l_x = lcopy(x_hbm.at[:, pl.ds(t * 1024, 1024)], xv)
    l_down = lcopy(down_hbm, downv)

    lane = lax.broadcasted_iota(jnp.int32, (8, 128), 1)
    pos = jnp.zeros((8, 128), jnp.int32)
    for b in range(8):
        pos = jnp.where((lane >> 4) == b, tp_ref[owner_ref[b]], pos)
    meta_a[0] = pos
    meta_b[0] = pos

    pl.semaphore_wait(barrier, len(peers))

    qa = y * 4 + x
    qb = x * 4 + y
    w1 = []
    for d in (1, 2, 3):
        for rel in (0, 1):
            slot = (4 - d) * 2 + rel
            q = qa if slot < 5 else qb
            dst_t = ((z + d) % 4) * 2 + (c + rel) % 2
            w1.append(
                rcopy(
                    w_hbm.at[:, pl.ds(dst_t * 1024 + q * 64, 64), :],
                    wf.at[slot, :, pl.ds(q * 64, 64), :],
                    zdev(d, rel),
                )
            )
    m1 = []
    for d in (1, 2, 3):
        m1.append(rcopy(meta_a.at[0], meta_a.at[4 - d], xdev(d)))
        m1.append(rcopy(meta_b.at[0], meta_b.at[4 - d], ydev(d)))

    l_kvg.wait()
    l_up.wait()
    live = live_ref[0]
    for b in range(8):
        rows = pl.ds(b * 128, 128)
        upb = upv[owner_ref[b]]
        for ch in range(2):
            g = kvgv[ch, rows, :]
            g = jnp.where(b < live, g, jnp.zeros_like(g))
            gf[0, ch, rows, :] = g
            upart[b // 4, ch * 16:(ch + 1) * 16, (b % 4) * 128:(b % 4 + 1) * 128] = (
                lax.dot_general(upb[ch * 16:(ch + 1) * 16], g, NT, preferred_element_type=F32)
            )
    u1 = rcopy(upart.at[1 - c], urecv, sib)
    l_inner.wait()
    for b in range(8):
        rows = pl.ds(b * 128, 128)
        for ch, ag in ((0, aga), (1, agb)):
            ag[b * 16:(b + 1) * 16, 1024:1152] = jnp.dot(
                innerv[ch * 16:(ch + 1) * 16, b * 128:(b + 1) * 128], gf[0, ch, rows, :],
                preferred_element_type=F32,
            ).astype(BF)
    u1.wait_recv()
    uz[0] = (upart[c] + urecv[...]).astype(BF)
    u2 = [rcopy(uz.at[0], uz.at[4 - d], zdev(d, 0)) for d in (1, 3, 2)]
    g_r = rcopy(gf.at[0], gf.at[6], zdev(1, 0))
    g_l = rcopy(gf.at[0], gf.at[2], zdev(3, 0))
    g_s = [rcopy(gf.at[0], gf.at[1], sib)]

    for cp in w1:
        cp.wait_recv()
    half_a, half_b = pl.ds(2, 3), pl.ds(5, 3)

    def wslice(half, row, size):
        return wf.at[half, :, pl.ds(row, size), :]

    def own_send(half, row, size, dev):
        return rcopy(wslice(half, row, size), wslice(half, row, size), dev)

    wa_r = own_send(half_a, qa * 64, 64, xdev(1))
    wa_l = own_send(half_a, qa * 64, 64, xdev(3))
    wb_r = own_send(half_b, qb * 64, 64, ydev(1))
    wb_l = own_send(half_b, qb * 64, 64, ydev(3))
    w_s = rcopy(w_hbm.at[:, pl.ds(sib[1] * 1024, 1024), :], wf.at[1], sib)

    for cp in u2:
        cp.wait_recv()
    ubf[c] = (
        uz[0].astype(F32) + uz[1].astype(F32) + uz[2].astype(F32) + uz[3].astype(F32)
    ).astype(BF)
    u3 = rcopy(ubf.at[c], ubf.at[c], sib)

    xl, xr = (x + 3) % 4, (x + 1) % 4
    yd, yu = (y + 3) % 4, (y + 1) % 4
    wa_r.wait_recv()
    wa_l.wait_recv()
    wa_o1 = own_send(half_a, (y * 4 + xl) * 64, 32, xdev(1))
    wa_o2 = own_send(half_a, (y * 4 + xr) * 64 + 32, 32, xdev(3))
    wb_r.wait_recv()
    wb_l.wait_recv()
    wb_o1 = own_send(half_b, (x * 4 + yd) * 64, 32, ydev(1))
    wb_o2 = own_send(half_b, (x * 4 + yu) * 64 + 32, 32, ydev(3))

    u3.wait_recv()
    l_x.wait()
    for b in range(8):
        ub = ubf[b // 4, :, (b % 4) * 128:(b % 4 + 1) * 128]
        term = jnp.dot(ub, xv[b * 128:(b + 1) * 128, :], preferred_element_type=F32).astype(BF)
        aga[b * 16:(b + 1) * 16, 0:1024] = term[0:16]
        agb[b * 16:(b + 1) * 16, 0:1024] = term[16:32]

    def row(ref, start, size):
        return ref.at[pl.ds(start, size), :]

    a_r = rcopy(row(aga, 0, 128), row(aga, 384, 128), xdev(1))
    a_l = rcopy(row(aga, 0, 128), row(aga, 128, 128), xdev(3))
    b_r = rcopy(row(agb, 0, 128), row(agb, 384, 128), ydev(1))
    b_l = rcopy(row(agb, 0, 128), row(agb, 128, 128), ydev(3))

    wa_o1.wait_recv()
    wa_o2.wait_recv()
    wa2_r = own_send(half_a, y * 256, 256, ydev(1))
    wa2_l = own_send(half_a, y * 256, 256, ydev(3))
    wb_o1.wait_recv()
    wb_o2.wait_recv()
    wb2_r = own_send(half_b, x * 256, 256, xdev(1))
    wb2_l = own_send(half_b, x * 256, 256, xdev(3))

    for cp in m1:
        cp.wait_recv()
    out_row = lax.broadcasted_iota(jnp.int32, (512, 128), 0)
    lane1 = lax.broadcasted_iota(jnp.int32, (1, 128), 1)
    for s in range(4):
        for meta, e, ring, other, mine in (
            (meta_a, ea, 0, 2, (x, y)), (meta_b, eb, 2, 0, (y, x)),
        ):
            p = meta[s, 0:1, :]
            owner = p >> 3
            valid = ((owner >> ring) & 3) == mine[0]
            dest = (((owner >> other) & 3) - mine[1]) & 3
            target = jnp.where(valid, dest * 128 + (p & 7) * 16 + (lane1 & 15), -1)
            e[:, s * 128:(s + 1) * 128] = (out_row == target).astype(F32).astype(BF)

    l_down.wait()
    for b in range(8):
        asel[b * 32:(b + 1) * 32, :] = downv[owner_ref[b]]
        ub = 2.0 * ubf[b // 4, :, (b % 4) * 128:(b % 4 + 1) * 128].astype(F32)
        parts = []
        if b > 0:
            parts.append(jnp.zeros((b * 32, 128), F32))
        parts.append(ub)
        if b < 7:
            parts.append(jnp.zeros(((7 - b) * 32, 128), F32))
        ubd[b * 128:(b + 1) * 128, :] = jnp.concatenate(parts, axis=0).T.astype(BF)

    a_r.wait_recv()
    a_l.wait_recv()
    a_o1 = rcopy(row(aga, 384, 64), row(aga, 256, 64), xdev(1))
    a_o2 = rcopy(row(aga, 192, 64), row(aga, 320, 64), xdev(3))
    b_r.wait_recv()
    b_l.wait_recv()
    b_o1 = rcopy(row(agb, 384, 64), row(agb, 256, 64), ydev(1))
    b_o2 = rcopy(row(agb, 192, 64), row(agb, 320, 64), ydev(3))

    first, last = pl.ds(0, 512), pl.ds(512, 512)
    g_r.wait_recv()
    g_l.wait_recv()
    g_o1 = rcopy(gf.at[6, :, first, :], gf.at[4, :, first, :], zdev(1, 0))
    g_o2 = rcopy(gf.at[2, :, last, :], gf.at[4, :, last, :], zdev(3, 0))
    g_s.append(rcopy(gf.at[6], gf.at[7], sib))
    g_s.append(rcopy(gf.at[2], gf.at[3], sib))

    wa2_r.wait_recv()
    wa2_l.wait_recv()
    wa2_o1 = own_send(half_a, yd * 256, 128, ydev(1))
    wa2_o2 = own_send(half_a, yu * 256 + 128, 128, ydev(3))
    wb2_r.wait_recv()
    wb2_l.wait_recv()
    wb2_o1 = own_send(half_b, xl * 256, 128, xdev(1))
    wb2_o2 = own_send(half_b, xr * 256 + 128, 128, xdev(3))

    def gathered(e, ag, k):
        return jnp.dot(e[k * 128:(k + 1) * 128, :], ag[...], preferred_element_type=F32)

    rings = ((a_o1, a_o2, ea, aga, snd_a, r1_a, r2_a, own_a, dns_a, ydev),
             (b_o1, b_o2, eb, agb, snd_b, r1_b, r2_b, own_b, dns_b, xdev))
    steps = []
    for o1, o2, e, ag, snd, r1, r2, own, dns, dev in rings:
        o1.wait_recv()
        o2.wait_recv()
        snd[256:384, :] = gathered(e, ag, 2).astype(BF)
        s1 = rcopy(row(snd, 256, 64), row(r1, 0, 64), dev(1))
        s2 = rcopy(row(snd, 320, 64), row(r1, 64, 64), dev(3))
        up = gathered(e, ag, 1)
        snd[192:256, :] = up[64:128].astype(BF)
        dns[0:64, :] = up[0:64]
        s3 = rcopy(row(snd, 192, 64), row(r2, 64, 64), dev(1))
        dn = gathered(e, ag, 3)
        snd[384:448, :] = dn[0:64].astype(BF)
        dns[64:128, :] = dn[64:128]
        s4 = rcopy(row(snd, 384, 64), row(r2, 128, 64), dev(3))
        own[...] = gathered(e, ag, 0)
        steps.append((s1, s2, s3, s4))
    g_o1.wait_recv()
    g_o2.wait_recv()
    g_s.append(rcopy(gf.at[4], gf.at[5], sib))
    lasts = []
    for (s1, s2, s3, s4), (o1, o2, e, ag, snd, r1, r2, own, dns, dev) in zip(steps, rings):
        s1.wait_recv()
        snd[128:192, :] = (dns[0:64, :] + r1[0:64, :].astype(F32)).astype(BF)
        s5 = rcopy(row(snd, 128, 64), row(r2, 0, 64), dev(1))
        s2.wait_recv()
        snd[448:512, :] = (dns[64:128, :] + r1[64:128, :].astype(F32)).astype(BF)
        s6 = rcopy(row(snd, 448, 64), row(r2, 192, 64), dev(3))
        lasts.append((s3, s4, s5, s6))

    l_w.wait()
    w_s.wait_recv()
    for cp in (wa2_o1, wa2_o2, wb2_o1, wb2_o2, *g_s):
        cp.wait_recv()

    def tile(i, carry):
        cols = pl.ds(pl.multiple_of(i * 256, 256), 256)
        acc = jnp.dot(ubd[...], asel[:, cols], preferred_element_type=F32)
        lhs = jnp.concatenate([gf[s, ch] for s in range(8) for ch in range(2)], axis=1)
        rhs = jnp.concatenate([wf[s, ch, cols, :] for s in range(8) for ch in range(2)], axis=1)
        acc += lax.dot_general(lhs, rhs, NT, preferred_element_type=F32)
        hgv[:, cols] = acc.astype(BF)
        return carry

    lax.fori_loop(0, 4, tile, 0)
    o_h = lcopy(hgv, hg_hbm)

    for ch, (cps, (o1, o2, e, ag, snd, r1, r2, own, dns, dev)) in enumerate(zip(lasts, rings)):
        for cp in cps:
            cp.wait_recv()
        tot = 2.0 * (own[...] + r2[0:128, :].astype(F32) + r2[128:256, :].astype(F32))
        for q in range(8):
            gav[q, ch * 16:(ch + 1) * 16, :] = tot[q * 16:(q + 1) * 16, 0:1024]
            gbv[q, ch] = tot[q * 16:(q + 1) * 16, 1024:1152]
    o_a = lcopy(gav, ga_hbm)
    o_b = lcopy(gbv, gb_hbm)
    for cp in pending:
        cp.wait_send()
    o_h.wait()
    o_a.wait()
    o_b.wait()


def per_device(
    hidden_input,
    key_value_gradient,
    key_value_weight,
    down_adapters,
    up_adapters,
    adapter_inner_saved,
    block_owner_tenant,
    live_block_counts,
    tenant_position,
):
    hbm = pl.BlockSpec(memory_space=pltpu.HBM)
    smem = pl.BlockSpec(memory_space=pltpu.SMEM)
    v = pltpu.VMEM
    return pl.pallas_call(
        comm_kernel,
        out_shape=(
            jax.ShapeDtypeStruct((1024, 1024), BF),
            jax.ShapeDtypeStruct((8, 32, 1024), F32),
            jax.ShapeDtypeStruct((8, 2, 16, 128), F32),
        ),
        in_specs=[hbm] * 6 + [smem] * 3,
        out_specs=(hbm, hbm, hbm),
        scratch_shapes=[
            v((8, 2, 1024, 128), BF),
            v((8, 2, 1024, 128), BF),
            v((1024, 1024), BF),
            v((128, 32, 1024), BF),
            v((128, 32, 128), BF),
            v((32, 1024), BF),
            v((2, 1024, 128), BF),
            v((2, 32, 512), F32),
            v((32, 512), F32),
            v((4, 32, 512), BF),
            v((2, 32, 512), BF),
            v((1024, 256), BF),
            v((256, 1024), BF),
            v((4, 8, 128), jnp.int32),
            v((4, 8, 128), jnp.int32),
            v((512, 512), BF),
            v((512, 512), BF),
            v((512, 1152), BF),
            v((512, 1152), BF),
            v((512, 1152), BF),
            v((512, 1152), BF),
            v((128, 1152), BF),
            v((128, 1152), BF),
            v((256, 1152), BF),
            v((256, 1152), BF),
            v((128, 1152), F32),
            v((128, 1152), F32),
            v((128, 1152), F32),
            v((128, 1152), F32),
            v((1024, 1024), BF),
            v((8, 32, 1024), F32),
            v((8, 2, 16, 128), F32),
            pltpu.SemaphoreType.DMA((N_REMOTE,)),
            pltpu.SemaphoreType.DMA((N_REMOTE,)),
            pltpu.SemaphoreType.DMA((N_LOCAL,)),
        ],
        compiler_params=pltpu.CompilerParams(
            collective_id=0, has_side_effects=True, vmem_limit_bytes=56 * 1024 * 1024
        ),
        name="projection_backward",
    )(
        hidden_input, key_value_gradient, key_value_weight, down_adapters,
        up_adapters.reshape(128, 32, 128), adapter_inner_saved,
        block_owner_tenant, live_block_counts, tenant_position,
    )


def solution(mesh):
    return jax.shard_map(
        per_device,
        mesh=mesh,
        in_specs=(
            P("dp", None),
            P(None, "dp", "tensor"),
            P(None, None, "tensor"),
            P(None, None, "tensor"),
            P(None, None, None, "tensor"),
            P(None, "dp"),
            P("dp"),
            P("dp"),
            P(),
        ),
        out_specs=(P("dp", "tensor"), P("dp", None, "tensor"), P("dp", None, None, "tensor")),
        check_vma=False,
    )
```

```python
import jax
import jax.numpy as jnp
from jax import lax
from jax.experimental import pallas as pl
from jax.experimental.pallas import tpu as pltpu
from jax.sharding import PartitionSpec as P

MESH = pl.DeviceIdType.MESH
BF = jnp.bfloat16
F32 = jnp.float32
NT = (((1,), (1,)), ((), ()))
N_REMOTE = 100
N_LOCAL = 6


def comm_kernel(
    x_hbm, kvg_hbm, w_hbm, down_hbm, up_hbm, inner_hbm, owner_ref, live_ref, tp_ref,
    hg_out, ga_out, gb_out,
    gf, wf, xv, downv, upv, innerv, kvgv,
    upart, urecv, uz, ubf, ubd, asel,
    meta_a, meta_b, ea, eb, aga, agb,
    snd_a, snd_b, r1_a, r1_b, r2_a, r2_b, own_a, own_b, dns_a, dns_b,
    acc,
    ss, rs, ls,
):
    dp = lax.axis_index("dp")
    t = lax.axis_index("tensor")
    y, x = dp // 4, dp % 4
    z, c = t // 2, t % 2

    def xdev(d):
        return (y * 4 + (x + d) % 4, t)

    def ydev(d):
        return (((y + d) % 4) * 4 + x, t)

    def zdev(d, rel):
        return (dp, ((z + d) % 4) * 2 + (c + rel) % 2)

    sib = zdev(0, 1)
    count = [0, 0]
    pending = []

    def rcopy(src, dst, dev):
        k = count[0]
        count[0] += 1
        cp = pltpu.make_async_remote_copy(
            src_ref=src, dst_ref=dst, send_sem=ss.at[k], recv_sem=rs.at[k],
            device_id=dev, device_id_type=MESH,
        )
        cp.start()
        pending.append(cp)
        return cp

    def lcopy(src, dst):
        k = count[1]
        count[1] += 1
        cp = pltpu.make_async_copy(src, dst, ls.at[k])
        cp.start()
        return cp

    peers = [sib]
    peers += [zdev(d, rel) for d in (1, 2, 3) for rel in (0, 1)]
    peers += [xdev(d) for d in (1, 2, 3)] + [ydev(d) for d in (1, 2, 3)]
    barrier = pltpu.get_barrier_semaphore()
    for dev in peers:
        pl.semaphore_signal(barrier, inc=1, device_id=dev, device_id_type=MESH)

    l_kvg = lcopy(kvg_hbm, kvgv)
    l_up = lcopy(up_hbm, upv)
    l_inner = lcopy(inner_hbm, innerv)
    l_w = lcopy(w_hbm.at[:, pl.ds(t * 1024, 1024), :], wf.at[0])
    l_x = lcopy(x_hbm.at[:, pl.ds(t * 1024, 1024)], xv)
    l_down = lcopy(down_hbm, downv)

    lane = lax.broadcasted_iota(jnp.int32, (8, 128), 1)
    pos = jnp.zeros((8, 128), jnp.int32)
    for b in range(8):
        pos = jnp.where((lane >> 4) == b, tp_ref[owner_ref[b]], pos)
    meta_a[0] = pos
    meta_b[0] = pos

    pl.semaphore_wait(barrier, len(peers))

    qa = y * 4 + x
    qb = x * 4 + y
    w1 = []
    for d in (1, 3, 2):
        for rel in (0, 1):
            slot = (4 - d) * 2 + rel
            q = qa if slot < 5 else qb
            dst_t = ((z + d) % 4) * 2 + (c + rel) % 2
            w1.append(
                rcopy(
                    w_hbm.at[:, pl.ds(dst_t * 1024 + q * 64, 64), :],
                    wf.at[slot, :, pl.ds(q * 64, 64), :],
                    zdev(d, rel),
                )
            )
    m1 = []
    for d in (1, 2, 3):
        m1.append(rcopy(meta_a.at[0], meta_a.at[4 - d], xdev(d)))
        m1.append(rcopy(meta_b.at[0], meta_b.at[4 - d], ydev(d)))

    l_kvg.wait()
    l_up.wait()
    live = live_ref[0]
    for b in range(8):
        rows = pl.ds(b * 128, 128)
        upb = upv[owner_ref[b]]
        for ch in range(2):
            g = kvgv[ch, rows, :]
            g = jnp.where(b < live, g, jnp.zeros_like(g))
            gf[0, ch, rows, :] = g
            upart[b // 4, ch * 16:(ch + 1) * 16, (b % 4) * 128:(b % 4 + 1) * 128] = (
                lax.dot_general(upb[ch * 16:(ch + 1) * 16], g, NT, preferred_element_type=F32)
            )
    u1 = rcopy(upart.at[1 - c], urecv, sib)
    l_inner.wait()
    for b in range(8):
        rows = pl.ds(b * 128, 128)
        for ch, ag in ((0, aga), (1, agb)):
            ag[b * 16:(b + 1) * 16, 1024:1152] = jnp.dot(
                innerv[ch * 16:(ch + 1) * 16, b * 128:(b + 1) * 128], gf[0, ch, rows, :],
                preferred_element_type=F32,
            ).astype(BF)
    u1.wait_recv()
    uz[0] = (upart[c] + urecv[...]).astype(BF)
    u2 = [rcopy(uz.at[0], uz.at[4 - d], zdev(d, 0)) for d in (1, 3, 2)]
    first, last = pl.ds(0, 512), pl.ds(512, 512)

    def gsend(slot, dst, part, dev):
        return rcopy(gf.at[slot, :, part, :], gf.at[dst, :, part, :], dev)

    g_r1 = gsend(0, 6, first, zdev(1, 0))
    g_l1 = gsend(0, 2, last, zdev(3, 0))
    g_r2 = gsend(0, 6, last, zdev(1, 0))
    g_l2 = gsend(0, 2, first, zdev(3, 0))
    g_s = [rcopy(gf.at[0], gf.at[1], sib)]

    half_a, half_b = pl.ds(2, 3), pl.ds(5, 3)

    def wsend(half, row, size, devs):
        part = wf.at[half, :, pl.ds(row, size), :]
        return [rcopy(part, part, dev) for dev in devs]

    xs, ys = (xdev(1), xdev(3)), (ydev(1), ydev(3))
    for cp in w1:
        cp.wait_recv()
    wa1 = wsend(half_a, qa * 64, 64, xs)
    wb1 = wsend(half_b, qb * 64, 64, ys)
    w2a = wsend(half_a, qa * 64, 64, ys)
    w2b = wsend(half_b, qb * 64, 64, xs)
    w_s = rcopy(w_hbm.at[:, pl.ds(sib[1] * 1024, 1024), :], wf.at[1], sib)

    for cp in u2:
        cp.wait_recv()
    ubf[c] = (
        uz[0].astype(F32) + uz[1].astype(F32) + uz[2].astype(F32) + uz[3].astype(F32)
    ).astype(BF)
    u3 = rcopy(ubf.at[c], ubf.at[c], sib)

    l_x.wait()
    u3.wait_recv()
    for b in range(8):
        ub = ubf[b // 4, :, (b % 4) * 128:(b % 4 + 1) * 128]
        term = jnp.dot(ub, xv[b * 128:(b + 1) * 128, :], preferred_element_type=F32).astype(BF)
        aga[b * 16:(b + 1) * 16, 0:1024] = term[0:16]
        agb[b * 16:(b + 1) * 16, 0:1024] = term[16:32]

    def row(ref, start, size):
        return ref.at[pl.ds(start, size), :]

    a_r = rcopy(row(aga, 0, 128), row(aga, 384, 128), xdev(1))
    a_l = rcopy(row(aga, 0, 128), row(aga, 128, 128), xdev(3))
    b_r = rcopy(row(agb, 0, 128), row(agb, 384, 128), ydev(1))
    b_l = rcopy(row(agb, 0, 128), row(agb, 128, 128), ydev(3))

    xl, xr, xo = (x + 3) % 4, (x + 1) % 4, (x + 2) % 4
    yd, yu, yo = (y + 3) % 4, (y + 1) % 4, (y + 2) % 4
    for cp in wa1 + wb1:
        cp.wait_recv()
    wa1o = wsend(half_a, (y * 4 + xl) * 64, 32, xs[:1])
    wa1o += wsend(half_a, (y * 4 + xr) * 64 + 32, 32, xs[1:])
    wb1o = wsend(half_b, (x * 4 + yd) * 64, 32, ys[:1])
    wb1o += wsend(half_b, (x * 4 + yu) * 64 + 32, 32, ys[1:])
    w2a += wsend(half_a, (y * 4 + xl) * 64, 64, ys)
    w2b += wsend(half_b, (x * 4 + yd) * 64, 64, xs)

    for cp in m1:
        cp.wait_recv()
    out_row = lax.broadcasted_iota(jnp.int32, (512, 128), 0)
    lane1 = lax.broadcasted_iota(jnp.int32, (1, 128), 1)
    for s in range(4):
        for meta, e, ring, other, mine in (
            (meta_a, ea, 0, 2, (x, y)), (meta_b, eb, 2, 0, (y, x)),
        ):
            p = meta[s, 0:1, :]
            owner = p >> 3
            valid = ((owner >> ring) & 3) == mine[0]
            dest = (((owner >> other) & 3) - mine[1]) & 3
            target = jnp.where(valid, dest * 128 + (p & 7) * 16 + (lane1 & 15), -1)
            e[:, s * 128:(s + 1) * 128] = (out_row == target).astype(F32).astype(BF)

    l_down.wait()
    for b in range(8):
        asel[b * 32:(b + 1) * 32, :] = downv[owner_ref[b]]
        ub = 2.0 * ubf[b // 4, :, (b % 4) * 128:(b % 4 + 1) * 128].astype(F32)
        parts = []
        if b > 0:
            parts.append(jnp.zeros((b * 32, 128), F32))
        parts.append(ub)
        if b < 7:
            parts.append(jnp.zeros(((7 - b) * 32, 128), F32))
        ubd[b * 128:(b + 1) * 128, :] = jnp.concatenate(parts, axis=0).T.astype(BF)

    def product(slots, tile):
        start = pl.multiple_of(tile * 256, 256)
        pairs = [(s, ch) for s in slots for ch in range(2)]
        lhs = jnp.concatenate([gf[s, ch] for s, ch in pairs], axis=1)
        rhs = jnp.concatenate([wf[s, ch, pl.ds(start, 256), :] for s, ch in pairs], axis=1)
        return lax.dot_general(lhs, rhs, NT, preferred_element_type=F32)

    l_w.wait()
    w_s.wait_recv()
    g_s[0].wait_recv()

    def own_pass(i, carry):
        cols = pl.ds(pl.multiple_of(i * 256, 256), 256)
        acc[i] = product((0, 1), i) + jnp.dot(
            ubd[...], asel[:, cols], preferred_element_type=F32
        )
        return carry

    lax.fori_loop(0, 4, own_pass, 0)

    g_r1.wait_recv()
    g_l1.wait_recv()
    g_o = [gsend(6, 4, first, zdev(1, 0)), gsend(2, 4, last, zdev(3, 0))]
    w3 = []
    for d in (1, 3, 2):
        for rel in (0, 1):
            slot = (4 - d) * 2 + rel
            far = (yo if slot < 5 else xo) * 256
            dst_t = ((z + d) % 4) * 2 + (c + rel) % 2
            w3.append(
                rcopy(
                    w_hbm.at[:, pl.ds(dst_t * 1024 + far, 256), :],
                    wf.at[slot, :, pl.ds(far, 256), :],
                    zdev(d, rel),
                )
            )

    a_r.wait_recv()
    a_l.wait_recv()
    a_o1 = rcopy(row(aga, 384, 64), row(aga, 256, 64), xdev(1))
    a_o2 = rcopy(row(aga, 192, 64), row(aga, 320, 64), xdev(3))
    b_r.wait_recv()
    b_l.wait_recv()
    b_o1 = rcopy(row(agb, 384, 64), row(agb, 256, 64), ydev(1))
    b_o2 = rcopy(row(agb, 192, 64), row(agb, 320, 64), ydev(3))
    w2a += wsend(half_a, (y * 4 + xr) * 64, 64, ys)
    w2b += wsend(half_b, (x * 4 + yu) * 64, 64, xs)
    for cp in wa1o + wb1o:
        cp.wait_recv()
    w2a += wsend(half_a, (y * 4 + xo) * 64, 64, ys)
    w2b += wsend(half_b, (x * 4 + yo) * 64, 64, xs)
    g_r2.wait_recv()
    g_l2.wait_recv()
    g_s.append(rcopy(gf.at[6], gf.at[7], sib))
    g_s.append(rcopy(gf.at[2], gf.at[3], sib))
    for cp in g_o:
        cp.wait_recv()
    g_s.append(rcopy(gf.at[4], gf.at[5], sib))

    def gathered(e, ag, k, n=1):
        return jnp.dot(e[k * 128:(k + n) * 128, :], ag[...], preferred_element_type=F32)

    rings = ((a_o1, a_o2, ea, aga, snd_a, r1_a, r2_a, own_a, dns_a, ydev),
             (b_o1, b_o2, eb, agb, snd_b, r1_b, r2_b, own_b, dns_b, xdev))
    steps = []
    for o1, o2, e, ag, snd, r1, r2, own, dns, dev in rings:
        o1.wait_recv()
        o2.wait_recv()
        snd[256:384, :] = gathered(e, ag, 2).astype(BF)
        s1 = rcopy(row(snd, 256, 64), row(r1, 0, 64), dev(1))
        s2 = rcopy(row(snd, 320, 64), row(r1, 64, 64), dev(3))
        steps.append([s1, s2])
    for step, (o1, o2, e, ag, snd, r1, r2, own, dns, dev) in zip(steps, rings):
        dn = gathered(e, ag, 3)
        snd[384:448, :] = dn[0:64].astype(BF)
        dns[64:128, :] = dn[64:128]
        low = gathered(e, ag, 0, 2)
        own[...] = low[0:128]
        snd[192:256, :] = low[192:256].astype(BF)
        dns[0:64, :] = low[128:192]
        step.append(rcopy(row(snd, 192, 64), row(r2, 64, 64), dev(1)))
        step.append(rcopy(row(snd, 384, 64), row(r2, 128, 64), dev(3)))

    group_a, group_b = (2, 3, 4), (5, 6, 7)

    def near_pass(i, carry):
        ta, tb = (y + i) % 4, (x + i) % 4
        acc[ta] += product(group_a, ta)
        acc[tb] += product(group_b, tb)
        return carry

    for cp in g_s[1:]:
        cp.wait_recv()
    near_pass(0, 0)
    for cp in w2a + w2b:
        cp.wait_recv()

    def side_pass(i, carry):
        return near_pass(1 + 2 * i, carry)

    lax.fori_loop(0, 2, side_pass, 0)

    for step, (o1, o2, e, ag, snd, r1, r2, own, dns, dev) in zip(steps, rings):
        s1, s2, s3, s4 = step
        s1.wait_recv()
        snd[128:192, :] = (dns[0:64, :] + r1[0:64, :].astype(F32)).astype(BF)
        s5 = rcopy(row(snd, 128, 64), row(r2, 0, 64), dev(1))
        s2.wait_recv()
        snd[448:512, :] = (dns[64:128, :] + r1[64:128, :].astype(F32)).astype(BF)
        s6 = rcopy(row(snd, 448, 64), row(r2, 192, 64), dev(3))
        step += [s5, s6]

    for cp in w3:
        cp.wait_recv()
    near_pass(2, 0)
    for i in range(4):
        hg_out[:, i * 256:(i + 1) * 256] = acc[i].astype(BF)

    for ch, (step, (o1, o2, e, ag, snd, r1, r2, own, dns, dev)) in enumerate(zip(steps, rings)):
        for cp in step[2:]:
            cp.wait_recv()
        tot = 2.0 * (own[...] + r2[0:128, :].astype(F32) + r2[128:256, :].astype(F32))
        for q in range(8):
            ga_out[q, ch * 16:(ch + 1) * 16, :] = tot[q * 16:(q + 1) * 16, 0:1024]
            gb_out[q, ch] = tot[q * 16:(q + 1) * 16, 1024:1152]
    for cp in pending:
        cp.wait_send()


def store_kernel(hg, ga, gb, hg_hbm, ga_hbm, gb_hbm, sems):
    copies = [
        pltpu.make_async_copy(src, dst, sems.at[k])
        for k, (src, dst) in enumerate(((hg, hg_hbm), (ga, ga_hbm), (gb, gb_hbm)))
    ]
    for cp in copies:
        cp.start()
    for cp in copies:
        cp.wait()


def per_device(
    hidden_input,
    key_value_gradient,
    key_value_weight,
    down_adapters,
    up_adapters,
    adapter_inner_saved,
    block_owner_tenant,
    live_block_counts,
    tenant_position,
):
    hbm = pl.BlockSpec(memory_space=pltpu.HBM)
    smem = pl.BlockSpec(memory_space=pltpu.SMEM)
    v = pltpu.VMEM
    vmem = pl.BlockSpec(memory_space=pltpu.VMEM)
    vs = (pltpu.VMEM((1024, 1024), BF), pltpu.VMEM((8, 32, 1024), F32), pltpu.VMEM((8, 2, 16, 128), F32))
    shapes = (
        jax.ShapeDtypeStruct((1024, 1024), BF),
        jax.ShapeDtypeStruct((8, 32, 1024), F32),
        jax.ShapeDtypeStruct((8, 2, 16, 128), F32),
    )
    outs = pl.pallas_call(
        comm_kernel,
        out_shape=vs,
        in_specs=[hbm] * 6 + [smem] * 3,
        out_specs=(vmem, vmem, vmem),
        scratch_shapes=[
            v((8, 2, 1024, 128), BF),
            v((8, 2, 1024, 128), BF),
            v((1024, 1024), BF),
            v((128, 32, 1024), BF),
            v((128, 32, 128), BF),
            v((32, 1024), BF),
            v((2, 1024, 128), BF),
            v((2, 32, 512), F32),
            v((32, 512), F32),
            v((4, 32, 512), BF),
            v((2, 32, 512), BF),
            v((1024, 256), BF),
            v((256, 1024), BF),
            v((4, 8, 128), jnp.int32),
            v((4, 8, 128), jnp.int32),
            v((512, 512), BF),
            v((512, 512), BF),
            v((512, 1152), BF),
            v((512, 1152), BF),
            v((512, 1152), BF),
            v((512, 1152), BF),
            v((128, 1152), BF),
            v((128, 1152), BF),
            v((256, 1152), BF),
            v((256, 1152), BF),
            v((128, 1152), F32),
            v((128, 1152), F32),
            v((128, 1152), F32),
            v((128, 1152), F32),
            v((4, 1024, 256), F32),
            pltpu.SemaphoreType.DMA((N_REMOTE,)),
            pltpu.SemaphoreType.DMA((N_REMOTE,)),
            pltpu.SemaphoreType.DMA((N_LOCAL,)),
        ],
        compiler_params=pltpu.CompilerParams(
            collective_id=0, has_side_effects=True, vmem_limit_bytes=54 * 1024 * 1024
        ),
        name="projection_backward",
    )(
        hidden_input, key_value_gradient, key_value_weight, down_adapters,
        up_adapters.reshape(128, 32, 128), adapter_inner_saved,
        block_owner_tenant, live_block_counts, tenant_position,
    )
    return pl.pallas_call(
        store_kernel,
        out_shape=shapes,
        in_specs=[pl.BlockSpec(memory_space=pl.ANY)] * 3,
        out_specs=(hbm, hbm, hbm),
        scratch_shapes=[pltpu.SemaphoreType.DMA((3,))],
        name="store_outputs",
    )(*[pltpu.with_memory_space_constraint(o, pltpu.VMEM) for o in outs])


def solution(mesh):
    return jax.shard_map(
        per_device,
        mesh=mesh,
        in_specs=(
            P("dp", None),
            P(None, "dp", "tensor"),
            P(None, None, "tensor"),
            P(None, None, "tensor"),
            P(None, None, None, "tensor"),
            P(None, "dp"),
            P("dp"),
            P("dp"),
            P(),
        ),
        out_specs=(P("dp", "tensor"), P("dp", None, "tensor"), P("dp", None, None, "tensor")),
        check_vma=False,
    )
```

```python
import jax
import jax.numpy as jnp
from jax import lax
from jax.experimental import pallas as pl
from jax.experimental.pallas import tpu as pltpu
from jax.sharding import PartitionSpec as P

MESH = pl.DeviceIdType.MESH
BF = jnp.bfloat16
F32 = jnp.float32
NT = (((1,), (1,)), ((), ()))
N_REMOTE = 100
N_LOCAL = 6


def comm_kernel(
    x_hbm, kvg_hbm, w_hbm, down_hbm, up_hbm, inner_hbm, owner_ref, live_ref, tp_ref,
    hg_out, ga_out, gb_out,
    gf, wf, xv, downv, upv, innerv, kvgv,
    upart, urecv, uz, ubf, ubd, asel,
    meta_a, meta_b, ea, eb, aga, agb,
    snd_a, snd_b, r1_a, r1_b, r2_a, r2_b, own_a, own_b, dns_a, dns_b,
    acc,
    ss, rs, ls,
):
    dp = lax.axis_index("dp")
    t = lax.axis_index("tensor")
    y, x = dp // 4, dp % 4
    z, c = t // 2, t % 2

    def xdev(d):
        return (y * 4 + (x + d) % 4, t)

    def ydev(d):
        return (((y + d) % 4) * 4 + x, t)

    def zdev(d, rel):
        return (dp, ((z + d) % 4) * 2 + (c + rel) % 2)

    sib = zdev(0, 1)
    count = [0, 0]
    pending = []

    def rcopy(src, dst, dev):
        k = count[0]
        count[0] += 1
        cp = pltpu.make_async_remote_copy(
            src_ref=src, dst_ref=dst, send_sem=ss.at[k], recv_sem=rs.at[k],
            device_id=dev, device_id_type=MESH,
        )
        cp.start()
        pending.append(cp)
        return cp

    def lcopy(src, dst):
        k = count[1]
        count[1] += 1
        cp = pltpu.make_async_copy(src, dst, ls.at[k])
        cp.start()
        return cp

    peers = [sib]
    peers += [zdev(d, rel) for d in (1, 2, 3) for rel in (0, 1)]
    peers += [xdev(d) for d in (1, 2, 3)] + [ydev(d) for d in (1, 2, 3)]
    barrier = pltpu.get_barrier_semaphore()
    for dev in peers:
        pl.semaphore_signal(barrier, inc=1, device_id=dev, device_id_type=MESH)

    l_kvg = lcopy(kvg_hbm, kvgv)
    l_up = lcopy(up_hbm, upv)
    l_inner = lcopy(inner_hbm, innerv)

    lane = lax.broadcasted_iota(jnp.int32, (8, 128), 1)
    pos = jnp.zeros((8, 128), jnp.int32)
    for b in range(8):
        pos = jnp.where((lane >> 4) == b, tp_ref[owner_ref[b]], pos)
    meta_a[0] = pos
    meta_b[0] = pos

    pl.semaphore_wait(barrier, len(peers))

    qa = y * 4 + x
    qb = x * 4 + y
    w1 = []
    for d in (1, 3, 2):
        for rel in (0, 1):
            slot = (4 - d) * 2 + rel
            q = qa if slot < 5 else qb
            dst_t = ((z + d) % 4) * 2 + (c + rel) % 2
            w1.append(
                rcopy(
                    w_hbm.at[:, pl.ds(dst_t * 1024 + q * 64, 64), :],
                    wf.at[slot, :, pl.ds(q * 64, 64), :],
                    zdev(d, rel),
                )
            )
    m1 = []
    for d in (1, 2, 3):
        m1.append(rcopy(meta_a.at[0], meta_a.at[4 - d], xdev(d)))
        m1.append(rcopy(meta_b.at[0], meta_b.at[4 - d], ydev(d)))
    l_x = lcopy(x_hbm.at[:, pl.ds(t * 1024, 1024)], xv)

    l_kvg.wait()
    l_up.wait()
    live = live_ref[0]
    off = jnp.zeros((16, 128), BF)
    for b in range(8):
        rows = pl.ds(b * 128, 128)
        upb = upv[owner_ref[b]]
        up2 = jnp.concatenate(
            [jnp.concatenate([upb[0:16], off], axis=1), jnp.concatenate([off, upb[16:32]], axis=1)],
            axis=0,
        )
        g2 = []
        for ch in range(2):
            g = kvgv[ch, rows, :]
            g2.append(jnp.where(b < live, g, jnp.zeros_like(g)))
            gf[0, ch, rows, :] = g2[ch]
        upart[b // 4, :, (b % 4) * 128:(b % 4 + 1) * 128] = lax.dot_general(
            up2, jnp.concatenate(g2, axis=1), NT, preferred_element_type=F32
        )
    u1 = rcopy(upart.at[1 - c], urecv, sib)
    l_inner.wait()
    for b in range(8):
        rows = pl.ds(b * 128, 128)
        for ch, ag in ((0, aga), (1, agb)):
            ag[b * 16:(b + 1) * 16, 1024:1152] = jnp.dot(
                innerv[ch * 16:(ch + 1) * 16, b * 128:(b + 1) * 128], gf[0, ch, rows, :],
                preferred_element_type=F32,
            ).astype(BF)

    def wsend(slots, row, size, devs):
        part = wf.at[slots, :, pl.ds(row, size), :]
        return [rcopy(part, part, dev) for dev in devs]

    xs, ys = (xdev(1), xdev(3)), (ydev(1), ydev(3))
    half_a, half_b = pl.ds(2, 3), pl.ds(5, 3)
    wa1, wb1, w2a, w2b = [], [], [], []

    def start_rings(slots_a, slots_b):
        wa1.extend(wsend(slots_a, qa * 64, 64, xs))
        wb1.extend(wsend(slots_b, qb * 64, 64, ys))
        w2a.extend(wsend(slots_a, qa * 64, 64, ys))
        w2b.extend(wsend(slots_b, qb * 64, 64, xs))

    u1.wait_recv()
    uz[0] = (upart[c] + urecv[...]).astype(BF)
    u2 = [rcopy(uz.at[0], uz.at[4 - d], zdev(d, 0)) for d in (1, 3, 2)]
    first, last = pl.ds(0, 512), pl.ds(512, 512)

    def gsend(slot, dst, part, dev):
        return rcopy(gf.at[slot, :, part, :], gf.at[dst, :, part, :], dev)

    g_r1 = gsend(0, 6, first, zdev(1, 0))
    g_l1 = gsend(0, 2, last, zdev(3, 0))
    g_r2 = gsend(0, 6, last, zdev(1, 0))
    g_l2 = gsend(0, 2, first, zdev(3, 0))
    for cp in w1[:4]:
        cp.wait_recv()
    start_rings(pl.ds(2, 2), pl.ds(6, 2))
    for cp in w1[4:]:
        cp.wait_recv()
    start_rings(pl.ds(4, 1), pl.ds(5, 1))
    l_w = lcopy(w_hbm.at[:, pl.ds(t * 1024, 1024), :], wf.at[0])
    l_down = lcopy(down_hbm, downv)

    for cp in u2:
        cp.wait_recv()
    ubf[c] = (
        uz[0].astype(F32) + uz[1].astype(F32) + uz[2].astype(F32) + uz[3].astype(F32)
    ).astype(BF)
    u3 = rcopy(ubf.at[c], ubf.at[c], sib)

    l_x.wait()
    u3.wait_recv()
    for b in range(8):
        ub = ubf[b // 4, :, (b % 4) * 128:(b % 4 + 1) * 128]
        term = jnp.dot(ub, xv[b * 128:(b + 1) * 128, :], preferred_element_type=F32).astype(BF)
        aga[b * 16:(b + 1) * 16, 0:1024] = term[0:16]
        agb[b * 16:(b + 1) * 16, 0:1024] = term[16:32]

    def row(ref, start, size):
        return ref.at[pl.ds(start, size), :]

    ag_1, ag_2 = [], []
    for ag, dev in ((aga, xdev), (agb, ydev)):
        ag_1.append(rcopy(row(ag, 0, 64), row(ag, 384, 64), dev(1)))
        ag_1.append(rcopy(row(ag, 64, 64), row(ag, 192, 64), dev(3)))
    for ag, dev in ((aga, xdev), (agb, ydev)):
        ag_2.append(rcopy(row(ag, 64, 64), row(ag, 448, 64), dev(1)))
        ag_2.append(rcopy(row(ag, 0, 64), row(ag, 128, 64), dev(3)))
    g_s = [rcopy(gf.at[0], gf.at[1], sib)]
    w_s = rcopy(w_hbm.at[:, pl.ds(sib[1] * 1024, 1024), :], wf.at[1], sib)

    xl, xr, xo = (x + 3) % 4, (x + 1) % 4, (x + 2) % 4
    yd, yu, yo = (y + 3) % 4, (y + 1) % 4, (y + 2) % 4
    for cp in wa1 + wb1:
        cp.wait_recv()
    wa1o = wsend(half_a, (y * 4 + xl) * 64, 32, xs[:1])
    wa1o += wsend(half_a, (y * 4 + xr) * 64 + 32, 32, xs[1:])
    wb1o = wsend(half_b, (x * 4 + yd) * 64, 32, ys[:1])
    wb1o += wsend(half_b, (x * 4 + yu) * 64 + 32, 32, ys[1:])

    for cp in m1:
        cp.wait_recv()
    out_row = lax.broadcasted_iota(jnp.int32, (512, 128), 0)
    lane1 = lax.broadcasted_iota(jnp.int32, (1, 128), 1)
    for s in range(4):
        for meta, e, ring, other, mine in (
            (meta_a, ea, 0, 2, (x, y)), (meta_b, eb, 2, 0, (y, x)),
        ):
            p = meta[s, 0:1, :]
            owner = p >> 3
            valid = ((owner >> ring) & 3) == mine[0]
            dest = (((owner >> other) & 3) - mine[1]) & 3
            target = jnp.where(valid, dest * 128 + (p & 7) * 16 + (lane1 & 15), -1)
            e[:, s * 128:(s + 1) * 128] = (out_row == target).astype(F32).astype(BF)

    l_down.wait()
    for b in range(8):
        asel[b * 32:(b + 1) * 32, :] = downv[owner_ref[b]]
        ub = 2.0 * ubf[b // 4, :, (b % 4) * 128:(b % 4 + 1) * 128].astype(F32)
        parts = []
        if b > 0:
            parts.append(jnp.zeros((b * 32, 128), F32))
        parts.append(ub)
        if b < 7:
            parts.append(jnp.zeros(((7 - b) * 32, 128), F32))
        ubd[b * 128:(b + 1) * 128, :] = jnp.concatenate(parts, axis=0).T.astype(BF)

    g_r1.wait_recv()
    g_l1.wait_recv()
    g_o = [gsend(6, 4, first, zdev(1, 0)), gsend(2, 4, last, zdev(3, 0))]
    w3 = []
    for d in (1, 3, 2):
        for rel in (0, 1):
            slot = (4 - d) * 2 + rel
            far = (yo if slot < 5 else xo) * 256
            dst_t = ((z + d) % 4) * 2 + (c + rel) % 2
            w3.append(
                rcopy(
                    w_hbm.at[:, pl.ds(dst_t * 1024 + far, 256), :],
                    wf.at[slot, :, pl.ds(far, 256), :],
                    zdev(d, rel),
                )
            )

    def product(slots, tile):
        start = pl.multiple_of(tile * 256, 256)
        pairs = [(s, ch) for s in slots for ch in range(2)]
        lhs = jnp.concatenate([gf[s, ch] for s, ch in pairs], axis=1)
        rhs = jnp.concatenate([wf[s, ch, pl.ds(start, 256), :] for s, ch in pairs], axis=1)
        return lax.dot_general(lhs, rhs, NT, preferred_element_type=F32)

    l_w.wait()
    w_s.wait_recv()
    g_s[0].wait_recv()

    def own_pass(i, carry):
        cols = pl.ds(pl.multiple_of(i * 256, 256), 256)
        acc[i] = product((0, 1), i) + jnp.dot(
            ubd[...], asel[:, cols], preferred_element_type=F32
        )
        return carry

    lax.fori_loop(0, 4, own_pass, 0)

    for cp in ag_1:
        cp.wait_recv()
    a_o1 = rcopy(row(aga, 384, 64), row(aga, 256, 64), xdev(1))
    a_o2 = rcopy(row(aga, 192, 64), row(aga, 320, 64), xdev(3))
    b_o1 = rcopy(row(agb, 384, 64), row(agb, 256, 64), ydev(1))
    b_o2 = rcopy(row(agb, 192, 64), row(agb, 320, 64), ydev(3))
    w2a += wsend(half_a, (y * 4 + xl) * 64, 64, ys)
    w2b += wsend(half_b, (x * 4 + yd) * 64, 64, xs)
    w2a += wsend(half_a, (y * 4 + xr) * 64, 64, ys)
    w2b += wsend(half_b, (x * 4 + yu) * 64, 64, xs)
    for cp in wa1o + wb1o:
        cp.wait_recv()
    w2a += wsend(half_a, (y * 4 + xo) * 64, 64, ys)
    w2b += wsend(half_b, (x * 4 + yo) * 64, 64, xs)
    g_r2.wait_recv()
    g_l2.wait_recv()
    g_s.append(rcopy(gf.at[6], gf.at[7], sib))
    g_s.append(rcopy(gf.at[2], gf.at[3], sib))

    def gathered(e, ag, k, n=1):
        return jnp.dot(e[k * 128:(k + n) * 128, :], ag[...], preferred_element_type=F32)

    rings = ((a_o1, a_o2, ea, aga, snd_a, r1_a, r2_a, own_a, dns_a, ydev),
             (b_o1, b_o2, eb, agb, snd_b, r1_b, r2_b, own_b, dns_b, xdev))
    steps = []
    for cp in ag_2:
        cp.wait_recv()
    for o1, o2, e, ag, snd, r1, r2, own, dns, dev in rings:
        o1.wait_recv()
        o2.wait_recv()
        snd[256:384, :] = gathered(e, ag, 2).astype(BF)
        s1 = rcopy(row(snd, 256, 64), row(r1, 0, 64), dev(1))
        s2 = rcopy(row(snd, 320, 64), row(r1, 64, 64), dev(3))
        steps.append([s1, s2])
    for step, (o1, o2, e, ag, snd, r1, r2, own, dns, dev) in zip(steps, rings):
        dn = gathered(e, ag, 3)
        snd[384:448, :] = dn[0:64].astype(BF)
        dns[64:128, :] = dn[64:128]
        low = gathered(e, ag, 0, 2)
        own[...] = low[0:128]
        snd[192:256, :] = low[192:256].astype(BF)
        dns[0:64, :] = low[128:192]
        step.append(rcopy(row(snd, 192, 64), row(r2, 64, 64), dev(1)))
        step.append(rcopy(row(snd, 384, 64), row(r2, 128, 64), dev(3)))

    for cp in g_o:
        cp.wait_recv()
    g_s.append(rcopy(gf.at[4], gf.at[5], sib))
    group_a, group_b = (2, 3, 4), (5, 6, 7)

    def near_pass(i, carry):
        ta, tb = (y + i) % 4, (x + i) % 4
        acc[ta] += product(group_a, ta)
        acc[tb] += product(group_b, tb)
        return carry

    for cp in g_s[1:]:
        cp.wait_recv()
    near_pass(0, 0)
    for cp in w2a + w2b:
        cp.wait_recv()

    def side_pass(i, carry):
        return near_pass(1 + 2 * i, carry)

    lax.fori_loop(0, 2, side_pass, 0)

    for step, (o1, o2, e, ag, snd, r1, r2, own, dns, dev) in zip(steps, rings):
        s1, s2, s3, s4 = step
        s1.wait_recv()
        snd[128:192, :] = (dns[0:64, :] + r1[0:64, :].astype(F32)).astype(BF)
        s5 = rcopy(row(snd, 128, 64), row(r2, 0, 64), dev(1))
        s2.wait_recv()
        snd[448:512, :] = (dns[64:128, :] + r1[64:128, :].astype(F32)).astype(BF)
        s6 = rcopy(row(snd, 448, 64), row(r2, 192, 64), dev(3))
        step += [s5, s6]

    for cp in w3:
        cp.wait_recv()
    near_pass(2, 0)
    for i in range(4):
        hg_out[:, i * 256:(i + 1) * 256] = acc[i].astype(BF)

    for ch, (step, (o1, o2, e, ag, snd, r1, r2, own, dns, dev)) in enumerate(zip(steps, rings)):
        for cp in step[2:]:
            cp.wait_recv()
        tot = 2.0 * (own[...] + r2[0:128, :].astype(F32) + r2[128:256, :].astype(F32))
        for q in range(8):
            ga_out[q, ch * 16:(ch + 1) * 16, :] = tot[q * 16:(q + 1) * 16, 0:1024]
            gb_out[q, ch] = tot[q * 16:(q + 1) * 16, 1024:1152]
    for cp in pending:
        cp.wait_send()


def store_kernel(hg, ga, gb, hg_hbm, ga_hbm, gb_hbm, sems):
    parts = [(hg, hg_hbm, 256 * i, 256) for i in range(4)]
    parts += [(ga, ga_hbm, 4 * i, 4) for i in range(2)] + [(gb, gb_hbm, 0, 8)]
    copies = [
        pltpu.make_async_copy(src.at[pl.ds(at, size)], dst.at[pl.ds(at, size)], sems.at[k])
        for k, (src, dst, at, size) in enumerate(parts)
    ]
    for cp in copies:
        cp.start()
    for cp in copies:
        cp.wait()


def per_device(
    hidden_input,
    key_value_gradient,
    key_value_weight,
    down_adapters,
    up_adapters,
    adapter_inner_saved,
    block_owner_tenant,
    live_block_counts,
    tenant_position,
):
    hbm = pl.BlockSpec(memory_space=pltpu.HBM)
    smem = pl.BlockSpec(memory_space=pltpu.SMEM)
    v = pltpu.VMEM
    vmem = pl.BlockSpec(memory_space=pltpu.VMEM)
    vs = (pltpu.VMEM((1024, 1024), BF), pltpu.VMEM((8, 32, 1024), F32), pltpu.VMEM((8, 2, 16, 128), F32))
    shapes = (
        jax.ShapeDtypeStruct((1024, 1024), BF),
        jax.ShapeDtypeStruct((8, 32, 1024), F32),
        jax.ShapeDtypeStruct((8, 2, 16, 128), F32),
    )
    outs = pl.pallas_call(
        comm_kernel,
        out_shape=vs,
        in_specs=[hbm] * 6 + [smem] * 3,
        out_specs=(vmem, vmem, vmem),
        scratch_shapes=[
            v((8, 2, 1024, 128), BF),
            v((8, 2, 1024, 128), BF),
            v((1024, 1024), BF),
            v((128, 32, 1024), BF),
            v((128, 32, 128), BF),
            v((32, 1024), BF),
            v((2, 1024, 128), BF),
            v((2, 32, 512), F32),
            v((32, 512), F32),
            v((4, 32, 512), BF),
            v((2, 32, 512), BF),
            v((1024, 256), BF),
            v((256, 1024), BF),
            v((4, 8, 128), jnp.int32),
            v((4, 8, 128), jnp.int32),
            v((512, 512), BF),
            v((512, 512), BF),
            v((512, 1152), BF),
            v((512, 1152), BF),
            v((512, 1152), BF),
            v((512, 1152), BF),
            v((128, 1152), BF),
            v((128, 1152), BF),
            v((256, 1152), BF),
            v((256, 1152), BF),
            v((128, 1152), F32),
            v((128, 1152), F32),
            v((128, 1152), F32),
            v((128, 1152), F32),
            v((4, 1024, 256), F32),
            pltpu.SemaphoreType.DMA((N_REMOTE,)),
            pltpu.SemaphoreType.DMA((N_REMOTE,)),
            pltpu.SemaphoreType.DMA((N_LOCAL,)),
        ],
        compiler_params=pltpu.CompilerParams(
            collective_id=0, has_side_effects=True, vmem_limit_bytes=54 * 1024 * 1024
        ),
        name="projection_backward",
    )(
        hidden_input, key_value_gradient, key_value_weight, down_adapters,
        up_adapters.reshape(128, 32, 128), adapter_inner_saved,
        block_owner_tenant, live_block_counts, tenant_position,
    )
    return pl.pallas_call(
        store_kernel,
        out_shape=shapes,
        in_specs=[pl.BlockSpec(memory_space=pl.ANY)] * 3,
        out_specs=(hbm, hbm, hbm),
        scratch_shapes=[pltpu.SemaphoreType.DMA((7,))],
        name="store_outputs",
    )(*[pltpu.with_memory_space_constraint(o, pltpu.VMEM) for o in outs])


def solution(mesh):
    return jax.shard_map(
        per_device,
        mesh=mesh,
        in_specs=(
            P("dp", None),
            P(None, "dp", "tensor"),
            P(None, None, "tensor"),
            P(None, None, "tensor"),
            P(None, None, None, "tensor"),
            P(None, "dp"),
            P("dp"),
            P("dp"),
            P(),
        ),
        out_specs=(P("dp", "tensor"), P("dp", None, "tensor"), P("dp", None, None, "tensor")),
        check_vma=False,
    )
```

```python
import jax
import jax.numpy as jnp
from jax import lax
from jax.experimental import pallas as pl
from jax.experimental.pallas import tpu as pltpu
from jax.sharding import PartitionSpec as P

MESH = pl.DeviceIdType.MESH
BF = jnp.bfloat16
F32 = jnp.float32
NT = (((1,), (1,)), ((), ()))
N_REMOTE = 136
N_LOCAL = 6


def comm_kernel(
    x_hbm, kvg_hbm, w_hbm, down_hbm, up_hbm, inner_hbm, owner_ref, live_ref, tp_ref,
    hg_out, ga_out, gb_out,
    gf, wf, xv, downv, upv, innerv, kvgv,
    upart, urecv, uz, ubf, ubd, asel,
    meta_a, meta_b, ea, eb, aga, agb,
    snd_a, snd_b, r1_a, r1_b, r2_a, r2_b, own_a, own_b, dns_a, dns_b,
    acc,
    ss, rs, ls,
):
    dp = lax.axis_index("dp")
    t = lax.axis_index("tensor")
    y, x = dp // 4, dp % 4
    z, c = t // 2, t % 2

    def xdev(d):
        return (y * 4 + (x + d) % 4, t)

    def ydev(d):
        return (((y + d) % 4) * 4 + x, t)

    def zdev(d, rel):
        return (dp, ((z + d) % 4) * 2 + (c + rel) % 2)

    sib = zdev(0, 1)
    count = [0, 0]
    pending = []

    def rcopy(src, dst, dev):
        k = count[0]
        count[0] += 1
        cp = pltpu.make_async_remote_copy(
            src_ref=src, dst_ref=dst, send_sem=ss.at[k], recv_sem=rs.at[k],
            device_id=dev, device_id_type=MESH,
        )
        cp.start()
        pending.append(cp)
        return cp

    def lcopy(src, dst):
        k = count[1]
        count[1] += 1
        cp = pltpu.make_async_copy(src, dst, ls.at[k])
        cp.start()
        return cp

    peers = [sib]
    peers += [zdev(d, rel) for d in (1, 2, 3) for rel in (0, 1)]
    peers += [xdev(d) for d in (1, 2, 3)] + [ydev(d) for d in (1, 2, 3)]
    barrier = pltpu.get_barrier_semaphore()
    for dev in peers:
        pl.semaphore_signal(barrier, inc=1, device_id=dev, device_id_type=MESH)

    l_kvg = lcopy(kvg_hbm, kvgv)
    l_up = lcopy(up_hbm, upv)
    l_inner = lcopy(inner_hbm, innerv)

    lane = lax.broadcasted_iota(jnp.int32, (8, 128), 1)
    pos = jnp.zeros((8, 128), jnp.int32)
    for b in range(8):
        pos = jnp.where((lane >> 4) == b, tp_ref[owner_ref[b]], pos)
    meta_a[0] = pos
    meta_b[0] = pos

    pl.semaphore_wait(barrier, len(peers))

    qa = y * 4 + x
    qb = x * 4 + y
    w1 = []
    for d, rel in ((1, 0), (3, 0), (1, 1), (3, 1), (2, 0), (2, 1)):
        slot = (4 - d) * 2 + rel
        q = qa if slot < 5 else qb
        dst_t = ((z + d) % 4) * 2 + (c + rel) % 2
        w1.append(
            rcopy(
                w_hbm.at[:, pl.ds(dst_t * 1024 + q * 64, 64), :],
                wf.at[slot, :, pl.ds(q * 64, 64), :],
                zdev(d, rel),
            )
        )
    m1 = []
    for d in (1, 2, 3):
        m1.append(rcopy(meta_a.at[0], meta_a.at[4 - d], xdev(d)))
        m1.append(rcopy(meta_b.at[0], meta_b.at[4 - d], ydev(d)))
    l_x = lcopy(x_hbm.at[:, pl.ds(t * 1024, 1024)], xv)

    l_kvg.wait()
    l_up.wait()
    live = live_ref[0]
    off = jnp.zeros((16, 128), BF)
    for b in range(8):
        rows = pl.ds(b * 128, 128)
        upb = upv[owner_ref[b]]
        up2 = jnp.concatenate(
            [jnp.concatenate([upb[0:16], off], axis=1), jnp.concatenate([off, upb[16:32]], axis=1)],
            axis=0,
        )
        g2 = []
        for ch in range(2):
            g = kvgv[ch, rows, :]
            g2.append(jnp.where(b < live, g, jnp.zeros_like(g)))
            gf[0, ch, rows, :] = g2[ch]
        upart[b // 4, :, (b % 4) * 128:(b % 4 + 1) * 128] = lax.dot_general(
            up2, jnp.concatenate(g2, axis=1), NT, preferred_element_type=F32
        )
    u1 = rcopy(upart.at[1 - c], urecv, sib)
    l_inner.wait()
    for b in range(8):
        rows = pl.ds(b * 128, 128)
        for ch, ag in ((0, aga), (1, agb)):
            ag[b * 16:(b + 1) * 16, 1024:1152] = jnp.dot(
                innerv[ch * 16:(ch + 1) * 16, b * 128:(b + 1) * 128], gf[0, ch, rows, :],
                preferred_element_type=F32,
            ).astype(BF)

    def row(ref, start, size, cols=slice(None)):
        return ref.at[pl.ds(start, size), cols]

    low, high = pl.ds(0, 1024), pl.ds(1024, 128)
    bg = []
    for ag, dev in ((aga, xdev), (agb, ydev)):
        bg.append(rcopy(row(ag, 0, 128, high), row(ag, 384, 128, high), dev(1)))
        bg.append(rcopy(row(ag, 0, 128, high), row(ag, 128, 128, high), dev(3)))

    def wsend(slots, row, size, devs):
        part = wf.at[slots, :, pl.ds(row, size), :]
        return [rcopy(part, part, dev) for dev in devs]

    xs, ys = (xdev(1), xdev(3)), (ydev(1), ydev(3))
    half_a, half_b = pl.ds(2, 3), pl.ds(5, 3)
    wa1, wb1, w2a, w2b = [], [], [], []

    def start_rings(slots_a, slots_b):
        wa1.extend(wsend(slots_a, qa * 64, 64, xs))
        wb1.extend(wsend(slots_b, qb * 64, 64, ys))
        w2a.extend(wsend(slots_a, qa * 64, 64, ys))
        w2b.extend(wsend(slots_b, qb * 64, 64, xs))

    u1.wait_recv()
    uz[0] = (upart[c] + urecv[...]).astype(BF)
    u2 = [rcopy(uz.at[0], uz.at[4 - d], zdev(d, 0)) for d in (1, 3, 2)]
    first, last = pl.ds(0, 512), pl.ds(512, 512)

    def gsend(slot, dst, part, dev):
        return rcopy(gf.at[slot, :, part, :], gf.at[dst, :, part, :], dev)

    g_r1 = gsend(0, 6, first, zdev(1, 0))
    g_l1 = gsend(0, 2, last, zdev(3, 0))
    g_r2 = gsend(0, 6, last, zdev(1, 0))
    g_l2 = gsend(0, 2, first, zdev(3, 0))
    for cp in w1[:2]:
        cp.wait_recv()
    start_rings(pl.ds(2, 1), pl.ds(6, 1))
    for cp in w1[2:4]:
        cp.wait_recv()
    start_rings(pl.ds(3, 1), pl.ds(7, 1))
    for cp in w1[4:]:
        cp.wait_recv()
    start_rings(pl.ds(4, 1), pl.ds(5, 1))
    l_w = lcopy(w_hbm.at[:, pl.ds(t * 1024, 1024), :], wf.at[0])
    l_down = lcopy(down_hbm, downv)

    for cp in u2:
        cp.wait_recv()
    ubf[c] = (
        uz[0].astype(F32) + uz[1].astype(F32) + uz[2].astype(F32) + uz[3].astype(F32)
    ).astype(BF)
    u3 = rcopy(ubf.at[c], ubf.at[c], sib)

    l_x.wait()
    u3.wait_recv()
    for b in range(8):
        ub = ubf[b // 4, :, (b % 4) * 128:(b % 4 + 1) * 128]
        term = jnp.dot(ub, xv[b * 128:(b + 1) * 128, :], preferred_element_type=F32).astype(BF)
        aga[b * 16:(b + 1) * 16, 0:1024] = term[0:16]
        agb[b * 16:(b + 1) * 16, 0:1024] = term[16:32]

    ag_1, ag_2 = [], []
    for ag, dev in ((aga, xdev), (agb, ydev)):
        ag_1.append(rcopy(row(ag, 0, 64, low), row(ag, 384, 64, low), dev(1)))
        ag_1.append(rcopy(row(ag, 64, 64, low), row(ag, 192, 64, low), dev(3)))
    for ag, dev in ((aga, xdev), (agb, ydev)):
        ag_2.append(rcopy(row(ag, 64, 64, low), row(ag, 448, 64, low), dev(1)))
        ag_2.append(rcopy(row(ag, 0, 64, low), row(ag, 128, 64, low), dev(3)))
    for cp in bg:
        cp.wait_recv()
    for ag, dev in ((aga, xdev), (agb, ydev)):
        ag_2.append(rcopy(row(ag, 384, 64, high), row(ag, 256, 64, high), dev(1)))
        ag_2.append(rcopy(row(ag, 192, 64, high), row(ag, 320, 64, high), dev(3)))
    g_s = [rcopy(gf.at[0], gf.at[1], sib)]
    w_s = rcopy(w_hbm.at[:, pl.ds(sib[1] * 1024, 1024), :], wf.at[1], sib)

    xl, xr, xo = (x + 3) % 4, (x + 1) % 4, (x + 2) % 4
    yd, yu, yo = (y + 3) % 4, (y + 1) % 4, (y + 2) % 4
    for cp in wa1 + wb1:
        cp.wait_recv()
    far_a, far_b = pl.ds(4, 1), pl.ds(5, 1)
    w1o = wsend(far_a, (y * 4 + xl) * 64, 32, xs[:1])
    w1o += wsend(far_a, (y * 4 + xr) * 64 + 32, 32, xs[1:])
    w1o += wsend(far_b, (x * 4 + yd) * 64, 32, ys[:1])
    w1o += wsend(far_b, (x * 4 + yu) * 64 + 32, 32, ys[1:])

    for cp in m1:
        cp.wait_recv()
    out_row = lax.broadcasted_iota(jnp.int32, (512, 128), 0)
    lane1 = lax.broadcasted_iota(jnp.int32, (1, 128), 1)
    for s in range(4):
        for meta, e, ring, other, mine in (
            (meta_a, ea, 0, 2, (x, y)), (meta_b, eb, 2, 0, (y, x)),
        ):
            p = meta[s, 0:1, :]
            owner = p >> 3
            valid = ((owner >> ring) & 3) == mine[0]
            dest = (((owner >> other) & 3) - mine[1]) & 3
            target = jnp.where(valid, dest * 128 + (p & 7) * 16 + (lane1 & 15), -1)
            e[:, s * 128:(s + 1) * 128] = (out_row == target).astype(F32).astype(BF)

    l_down.wait()
    for b in range(8):
        asel[b * 32:(b + 1) * 32, :] = downv[owner_ref[b]]
        ub = 2.0 * ubf[b // 4, :, (b % 4) * 128:(b % 4 + 1) * 128].astype(F32)
        parts = []
        if b > 0:
            parts.append(jnp.zeros((b * 32, 128), F32))
        parts.append(ub)
        if b < 7:
            parts.append(jnp.zeros(((7 - b) * 32, 128), F32))
        ubd[b * 128:(b + 1) * 128, :] = jnp.concatenate(parts, axis=0).T.astype(BF)

    g_r1.wait_recv()
    g_l1.wait_recv()
    g_o = [gsend(6, 4, first, zdev(1, 0)), gsend(2, 4, last, zdev(3, 0))]

    def near_send(row_a, row_b, size):
        sent = []
        for d in (1, 3):
            for rel in (0, 1):
                slot = (4 - d) * 2 + rel
                at = row_a if slot < 5 else row_b
                dst_t = ((z + d) % 4) * 2 + (c + rel) % 2
                sent.append(
                    rcopy(
                        w_hbm.at[:, pl.ds(dst_t * 1024 + at, size), :],
                        wf.at[slot, :, pl.ds(at, size), :],
                        zdev(d, rel),
                    )
                )
        return sent

    w3 = []
    for i in (0, 3, 1):
        w3.append(
            near_send((((y + i) % 4) * 4 + xo) * 64, (((x + i) % 4) * 4 + yo) * 64, 64)
        )
    w3.append(near_send(yo * 256, xo * 256, 256))

    def product(slots, tile):
        start = pl.multiple_of(tile * 256, 256)
        pairs = [(s, ch) for s in slots for ch in range(2)]
        lhs = jnp.concatenate([gf[s, ch] for s, ch in pairs], axis=1)
        rhs = jnp.concatenate([wf[s, ch, pl.ds(start, 256), :] for s, ch in pairs], axis=1)
        return lax.dot_general(lhs, rhs, NT, preferred_element_type=F32)

    l_w.wait()
    w_s.wait_recv()
    g_s[0].wait_recv()

    def own_pass(i, carry):
        cols = pl.ds(pl.multiple_of(i * 256, 256), 256)
        acc[i] = product((0, 1), i) + jnp.dot(
            ubd[...], asel[:, cols], preferred_element_type=F32
        )
        return carry

    lax.fori_loop(0, 4, own_pass, 0)

    for cp in ag_1:
        cp.wait_recv()
    a_o1 = rcopy(row(aga, 384, 64, low), row(aga, 256, 64, low), xdev(1))
    a_o2 = rcopy(row(aga, 192, 64, low), row(aga, 320, 64, low), xdev(3))
    b_o1 = rcopy(row(agb, 384, 64, low), row(agb, 256, 64, low), ydev(1))
    b_o2 = rcopy(row(agb, 192, 64, low), row(agb, 320, 64, low), ydev(3))
    w2a += wsend(half_a, (y * 4 + xl) * 64, 64, ys)
    w2b += wsend(half_b, (x * 4 + yd) * 64, 64, xs)
    w2a += wsend(half_a, (y * 4 + xr) * 64, 64, ys)
    w2b += wsend(half_b, (x * 4 + yu) * 64, 64, xs)
    for cp in w1o:
        cp.wait_recv()
    w2a += wsend(far_a, (y * 4 + xo) * 64, 64, ys)
    w2b += wsend(far_b, (x * 4 + yo) * 64, 64, xs)
    g_r2.wait_recv()
    g_l2.wait_recv()
    g_s.append(rcopy(gf.at[6], gf.at[7], sib))
    g_s.append(rcopy(gf.at[2], gf.at[3], sib))

    def gathered(e, ag, k, n=1):
        return jnp.dot(e[k * 128:(k + n) * 128, :], ag[...], preferred_element_type=F32)

    rings = ((a_o1, a_o2, ea, aga, snd_a, r1_a, r2_a, own_a, dns_a, ydev),
             (b_o1, b_o2, eb, agb, snd_b, r1_b, r2_b, own_b, dns_b, xdev))
    steps = []
    for cp in ag_2:
        cp.wait_recv()
    for o1, o2, e, ag, snd, r1, r2, own, dns, dev in rings:
        o1.wait_recv()
        o2.wait_recv()
        snd[256:384, :] = gathered(e, ag, 2).astype(BF)
        s1 = rcopy(row(snd, 256, 64), row(r1, 0, 64), dev(1))
        s2 = rcopy(row(snd, 320, 64), row(r1, 64, 64), dev(3))
        steps.append([s1, s2])
    for step, (o1, o2, e, ag, snd, r1, r2, own, dns, dev) in zip(steps, rings):
        dn = gathered(e, ag, 3)
        snd[384:448, :] = dn[0:64].astype(BF)
        dns[64:128, :] = dn[64:128]
        up = gathered(e, ag, 0, 2)
        own[...] = up[0:128]
        snd[192:256, :] = up[192:256].astype(BF)
        dns[0:64, :] = up[128:192]
        step.append(rcopy(row(snd, 192, 64), row(r2, 64, 64), dev(1)))
        step.append(rcopy(row(snd, 384, 64), row(r2, 128, 64), dev(3)))

    for cp in g_o:
        cp.wait_recv()
    g_s.append(rcopy(gf.at[4], gf.at[5], sib))
    group_a, group_b = (2, 3, 4), (5, 6, 7)

    def near_pass(i, carry):
        ta, tb = (y + i) % 4, (x + i) % 4
        acc[ta] += product(group_a, ta)
        acc[tb] += product(group_b, tb)
        return carry

    for cp in w2a + w2b:
        cp.wait_recv()
    w2o = wsend(far_a, yd * 256, 128, ys[:1]) + wsend(far_a, yu * 256 + 128, 128, ys[1:])
    w2o += wsend(far_b, xl * 256, 128, xs[:1]) + wsend(far_b, xr * 256 + 128, 128, xs[1:])

    for step, (o1, o2, e, ag, snd, r1, r2, own, dns, dev) in zip(steps, rings):
        s1, s2, s3, s4 = step
        s1.wait_recv()
        snd[128:192, :] = (dns[0:64, :] + r1[0:64, :].astype(F32)).astype(BF)
        s5 = rcopy(row(snd, 128, 64), row(r2, 0, 64), dev(1))
        s2.wait_recv()
        snd[448:512, :] = (dns[64:128, :] + r1[64:128, :].astype(F32)).astype(BF)
        s6 = rcopy(row(snd, 448, 64), row(r2, 192, 64), dev(3))
        step += [s5, s6]

    for cp in g_s[1:] + w3[0]:
        cp.wait_recv()
    near_pass(0, 0)
    for cp in w3[1] + w3[2]:
        cp.wait_recv()

    def side_pass(i, carry):
        return near_pass(1 + 2 * i, carry)

    lax.fori_loop(0, 2, side_pass, 0)

    for cp in w3[3] + w2o:
        cp.wait_recv()
    near_pass(2, 0)
    for i in range(4):
        hg_out[:, i * 256:(i + 1) * 256] = acc[i].astype(BF)

    for ch, (step, (o1, o2, e, ag, snd, r1, r2, own, dns, dev)) in enumerate(zip(steps, rings)):
        for cp in step[2:]:
            cp.wait_recv()
        tot = 2.0 * (own[...] + r2[0:128, :].astype(F32) + r2[128:256, :].astype(F32))
        for q in range(8):
            ga_out[q, ch * 16:(ch + 1) * 16, :] = tot[q * 16:(q + 1) * 16, 0:1024]
            gb_out[q, ch] = tot[q * 16:(q + 1) * 16, 1024:1152]
    for cp in pending:
        cp.wait_send()


def store_kernel(hg, ga, gb, hg_hbm, ga_hbm, gb_hbm, sems):
    parts = [(hg, hg_hbm, 256 * i, 256) for i in range(4)]
    parts += [(ga, ga_hbm, 4 * i, 4) for i in range(2)] + [(gb, gb_hbm, 0, 8)]
    copies = [
        pltpu.make_async_copy(src.at[pl.ds(at, size)], dst.at[pl.ds(at, size)], sems.at[k])
        for k, (src, dst, at, size) in enumerate(parts)
    ]
    for cp in copies:
        cp.start()
    for cp in copies:
        cp.wait()


def per_device(
    hidden_input,
    key_value_gradient,
    key_value_weight,
    down_adapters,
    up_adapters,
    adapter_inner_saved,
    block_owner_tenant,
    live_block_counts,
    tenant_position,
):
    hbm = pl.BlockSpec(memory_space=pltpu.HBM)
    smem = pl.BlockSpec(memory_space=pltpu.SMEM)
    v = pltpu.VMEM
    vmem = pl.BlockSpec(memory_space=pltpu.VMEM)
    vs = (pltpu.VMEM((1024, 1024), BF), pltpu.VMEM((8, 32, 1024), F32), pltpu.VMEM((8, 2, 16, 128), F32))
    shapes = (
        jax.ShapeDtypeStruct((1024, 1024), BF),
        jax.ShapeDtypeStruct((8, 32, 1024), F32),
        jax.ShapeDtypeStruct((8, 2, 16, 128), F32),
    )
    outs = pl.pallas_call(
        comm_kernel,
        out_shape=vs,
        in_specs=[hbm] * 6 + [smem] * 3,
        out_specs=(vmem, vmem, vmem),
        scratch_shapes=[
            v((8, 2, 1024, 128), BF),
            v((8, 2, 1024, 128), BF),
            v((1024, 1024), BF),
            v((128, 32, 1024), BF),
            v((128, 32, 128), BF),
            v((32, 1024), BF),
            v((2, 1024, 128), BF),
            v((2, 32, 512), F32),
            v((32, 512), F32),
            v((4, 32, 512), BF),
            v((2, 32, 512), BF),
            v((1024, 256), BF),
            v((256, 1024), BF),
            v((4, 8, 128), jnp.int32),
            v((4, 8, 128), jnp.int32),
            v((512, 512), BF),
            v((512, 512), BF),
            v((512, 1152), BF),
            v((512, 1152), BF),
            v((512, 1152), BF),
            v((512, 1152), BF),
            v((128, 1152), BF),
            v((128, 1152), BF),
            v((256, 1152), BF),
            v((256, 1152), BF),
            v((128, 1152), F32),
            v((128, 1152), F32),
            v((128, 1152), F32),
            v((128, 1152), F32),
            v((4, 1024, 256), F32),
            pltpu.SemaphoreType.DMA((N_REMOTE,)),
            pltpu.SemaphoreType.DMA((N_REMOTE,)),
            pltpu.SemaphoreType.DMA((N_LOCAL,)),
        ],
        compiler_params=pltpu.CompilerParams(
            collective_id=0, has_side_effects=True, vmem_limit_bytes=54 * 1024 * 1024
        ),
        name="projection_backward",
    )(
        hidden_input, key_value_gradient, key_value_weight, down_adapters,
        up_adapters.reshape(128, 32, 128), adapter_inner_saved,
        block_owner_tenant, live_block_counts, tenant_position,
    )
    return pl.pallas_call(
        store_kernel,
        out_shape=shapes,
        in_specs=[pl.BlockSpec(memory_space=pl.ANY)] * 3,
        out_specs=(hbm, hbm, hbm),
        scratch_shapes=[pltpu.SemaphoreType.DMA((7,))],
        name="store_outputs",
    )(*[pltpu.with_memory_space_constraint(o, pltpu.VMEM) for o in outs])


def solution(mesh):
    return jax.shard_map(
        per_device,
        mesh=mesh,
        in_specs=(
            P("dp", None),
            P(None, "dp", "tensor"),
            P(None, None, "tensor"),
            P(None, None, "tensor"),
            P(None, None, None, "tensor"),
            P(None, "dp"),
            P("dp"),
            P("dp"),
            P(),
        ),
        out_specs=(P("dp", "tensor"), P("dp", None, "tensor"), P("dp", None, None, "tensor")),
        check_vma=False,
    )
```

```python
import jax
import jax.numpy as jnp
from jax import lax
from jax.experimental import pallas as pl
from jax.experimental.pallas import tpu as pltpu
from jax.sharding import PartitionSpec as P

MESH = pl.DeviceIdType.MESH
BF = jnp.bfloat16
F32 = jnp.float32
NT = (((1,), (1,)), ((), ()))
N_REMOTE = 120
N_LOCAL = 6


def comm_kernel(
    x_hbm, kvg_hbm, w_hbm, down_hbm, up_hbm, inner_hbm, owner_ref, live_ref, tp_ref,
    hg_out, ga_out, gb_out,
    gf, wf, xv, downv, upv, innerv, kvgv,
    upart, urecv, uz, ubf, ubd, asel,
    meta_a, meta_b, ea, eb, aga, agb,
    snd_a, snd_b, r1_a, r1_b, r2_a, r2_b, own_a, own_b, dns_a, dns_b,
    acc,
    ss, rs, ls,
):
    dp = lax.axis_index("dp")
    t = lax.axis_index("tensor")
    y, x = dp // 4, dp % 4
    z, c = t // 2, t % 2

    def xdev(d):
        return (y * 4 + (x + d) % 4, t)

    def ydev(d):
        return (((y + d) % 4) * 4 + x, t)

    def zdev(d, rel):
        return (dp, ((z + d) % 4) * 2 + (c + rel) % 2)

    sib = zdev(0, 1)
    count = [0, 0]
    pending = []

    def rcopy(src, dst, dev):
        k = count[0]
        count[0] += 1
        cp = pltpu.make_async_remote_copy(
            src_ref=src, dst_ref=dst, send_sem=ss.at[k], recv_sem=rs.at[k],
            device_id=dev, device_id_type=MESH,
        )
        cp.start()
        pending.append(cp)
        return cp

    def lcopy(src, dst):
        k = count[1]
        count[1] += 1
        cp = pltpu.make_async_copy(src, dst, ls.at[k])
        cp.start()
        return cp

    peers = [sib]
    peers += [zdev(d, rel) for d in (1, 2, 3) for rel in (0, 1)]
    peers += [xdev(d) for d in (1, 2, 3)] + [ydev(d) for d in (1, 2, 3)]
    barrier = pltpu.get_barrier_semaphore()
    for dev in peers:
        pl.semaphore_signal(barrier, inc=1, device_id=dev, device_id_type=MESH)

    l_kvg = lcopy(kvg_hbm, kvgv)
    l_up = lcopy(up_hbm, upv)
    l_inner = lcopy(inner_hbm, innerv)

    lane = lax.broadcasted_iota(jnp.int32, (8, 128), 1)
    pos = jnp.zeros((8, 128), jnp.int32)
    for b in range(8):
        pos = jnp.where((lane >> 4) == b, tp_ref[owner_ref[b]], pos)
    meta_a[0] = pos
    meta_b[0] = pos

    pl.semaphore_wait(barrier, len(peers))

    qa = y * 4 + x
    qb = x * 4 + y
    w1 = []
    for d, rel in ((1, 0), (3, 0), (1, 1), (3, 1), (2, 0), (2, 1)):
        slot = (4 - d) * 2 + rel
        q = qa if slot < 5 else qb
        dst_t = ((z + d) % 4) * 2 + (c + rel) % 2
        w1.append(
            rcopy(
                w_hbm.at[:, pl.ds(dst_t * 1024 + q * 64, 64), :],
                wf.at[slot, :, pl.ds(q * 64, 64), :],
                zdev(d, rel),
            )
        )
    m1 = []
    for d in (1, 2, 3):
        m1.append(rcopy(meta_a.at[0], meta_a.at[4 - d], xdev(d)))
        m1.append(rcopy(meta_b.at[0], meta_b.at[4 - d], ydev(d)))
    l_x = lcopy(x_hbm.at[:, pl.ds(t * 1024, 1024)], xv)

    l_kvg.wait()
    l_up.wait()
    live = live_ref[0]
    off = jnp.zeros((16, 128), BF)
    for b in range(8):
        rows = pl.ds(b * 128, 128)
        upb = upv[owner_ref[b]]
        up2 = jnp.concatenate(
            [jnp.concatenate([upb[0:16], off], axis=1), jnp.concatenate([off, upb[16:32]], axis=1)],
            axis=0,
        )
        g2 = []
        for ch in range(2):
            g = kvgv[ch, rows, :]
            g2.append(jnp.where(b < live, g, jnp.zeros_like(g)))
            gf[0, ch, rows, :] = g2[ch]
        upart[b // 4, :, (b % 4) * 128:(b % 4 + 1) * 128] = lax.dot_general(
            up2, jnp.concatenate(g2, axis=1), NT, preferred_element_type=F32
        )
    u1 = rcopy(upart.at[1 - c], urecv, sib)
    l_inner.wait()
    for b in range(8):
        rows = pl.ds(b * 128, 128)
        for ch, ag in ((0, aga), (1, agb)):
            ag[b * 16:(b + 1) * 16, 1024:1152] = jnp.dot(
                innerv[ch * 16:(ch + 1) * 16, b * 128:(b + 1) * 128], gf[0, ch, rows, :],
                preferred_element_type=F32,
            ).astype(BF)

    def row(ref, start, size, cols=slice(None)):
        return ref.at[pl.ds(start, size), cols]

    low, high = pl.ds(0, 1024), pl.ds(1024, 128)
    bg = []
    for ag, dev in ((aga, xdev), (agb, ydev)):
        bg.append(rcopy(row(ag, 0, 128, high), row(ag, 384, 128, high), dev(1)))
        bg.append(rcopy(row(ag, 0, 128, high), row(ag, 128, 128, high), dev(3)))

    def wsend(slots, row, size, devs):
        part = wf.at[slots, :, pl.ds(row, size), :]
        return [rcopy(part, part, dev) for dev in devs]

    xs, ys = (xdev(1), xdev(3)), (ydev(1), ydev(3))
    half_a, half_b = pl.ds(2, 3), pl.ds(5, 3)
    wa1, wb1, w2a, w2b = [], [], [], []

    def start_rings(slots_a, slots_b):
        wa1.extend(wsend(slots_a, qa * 64, 64, xs))
        wb1.extend(wsend(slots_b, qb * 64, 64, ys))
        w2a.extend(wsend(slots_a, qa * 64, 64, ys))
        w2b.extend(wsend(slots_b, qb * 64, 64, xs))

    u1.wait_recv()
    uz[0] = (upart[c] + urecv[...]).astype(BF)
    u2 = [rcopy(uz.at[0], uz.at[4 - d], zdev(d, 0)) for d in (1, 3, 2)]
    first, last = pl.ds(0, 512), pl.ds(512, 512)

    def gsend(slot, dst, part, dev):
        return rcopy(gf.at[slot, :, part, :], gf.at[dst, :, part, :], dev)

    g_r1 = gsend(0, 6, first, zdev(1, 0))
    g_l1 = gsend(0, 2, last, zdev(3, 0))
    g_r2 = gsend(0, 6, last, zdev(1, 0))
    g_l2 = gsend(0, 2, first, zdev(3, 0))
    for cp in w1[:2]:
        cp.wait_recv()
    start_rings(pl.ds(2, 1), pl.ds(6, 1))
    for cp in w1[2:4]:
        cp.wait_recv()
    start_rings(pl.ds(3, 1), pl.ds(7, 1))
    for cp in w1[4:]:
        cp.wait_recv()
    start_rings(pl.ds(4, 1), pl.ds(5, 1))
    l_w = lcopy(w_hbm.at[:, pl.ds(t * 1024, 1024), :], wf.at[0])
    l_down = lcopy(down_hbm, downv)

    for cp in u2:
        cp.wait_recv()
    ubf[c] = (
        uz[0].astype(F32) + uz[1].astype(F32) + uz[2].astype(F32) + uz[3].astype(F32)
    ).astype(BF)
    u3 = rcopy(ubf.at[c], ubf.at[c], sib)

    l_x.wait()
    u3.wait_recv()
    for b in range(8):
        ub = ubf[b // 4, :, (b % 4) * 128:(b % 4 + 1) * 128]
        term = jnp.dot(ub, xv[b * 128:(b + 1) * 128, :], preferred_element_type=F32).astype(BF)
        aga[b * 16:(b + 1) * 16, 0:1024] = term[0:16]
        agb[b * 16:(b + 1) * 16, 0:1024] = term[16:32]

    ag_1, ag_2 = [], []
    for ag, dev in ((aga, xdev), (agb, ydev)):
        ag_1.append(rcopy(row(ag, 0, 64, low), row(ag, 384, 64, low), dev(1)))
        ag_1.append(rcopy(row(ag, 64, 64, low), row(ag, 192, 64, low), dev(3)))
    for ag, dev in ((aga, xdev), (agb, ydev)):
        ag_2.append(rcopy(row(ag, 64, 64, low), row(ag, 448, 64, low), dev(1)))
        ag_2.append(rcopy(row(ag, 0, 64, low), row(ag, 128, 64, low), dev(3)))
    for cp in bg:
        cp.wait_recv()
    for ag, dev in ((aga, xdev), (agb, ydev)):
        ag_2.append(rcopy(row(ag, 384, 64, high), row(ag, 256, 64, high), dev(1)))
        ag_2.append(rcopy(row(ag, 192, 64, high), row(ag, 320, 64, high), dev(3)))
    g_s = [rcopy(gf.at[0], gf.at[1], sib)]
    w_s = rcopy(w_hbm.at[:, pl.ds(sib[1] * 1024, 1024), :], wf.at[1], sib)

    xl, xr, xo = (x + 3) % 4, (x + 1) % 4, (x + 2) % 4
    yd, yu, yo = (y + 3) % 4, (y + 1) % 4, (y + 2) % 4
    for cp in wa1 + wb1:
        cp.wait_recv()
    far_a, far_b = pl.ds(4, 1), pl.ds(5, 1)
    w1o = wsend(far_a, (y * 4 + xl) * 64, 32, xs[:1])
    w1o += wsend(far_a, (y * 4 + xr) * 64 + 32, 32, xs[1:])
    w1o += wsend(far_b, (x * 4 + yd) * 64, 32, ys[:1])
    w1o += wsend(far_b, (x * 4 + yu) * 64 + 32, 32, ys[1:])

    for cp in m1:
        cp.wait_recv()
    out_row = lax.broadcasted_iota(jnp.int32, (512, 128), 0)
    lane1 = lax.broadcasted_iota(jnp.int32, (1, 128), 1)
    for s in range(4):
        for meta, e, ring, other, mine in (
            (meta_a, ea, 0, 2, (x, y)), (meta_b, eb, 2, 0, (y, x)),
        ):
            p = meta[s, 0:1, :]
            owner = p >> 3
            valid = ((owner >> ring) & 3) == mine[0]
            dest = (((owner >> other) & 3) - mine[1]) & 3
            target = jnp.where(valid, dest * 128 + (p & 7) * 16 + (lane1 & 15), -1)
            e[:, s * 128:(s + 1) * 128] = (out_row == target).astype(F32).astype(BF)

    l_down.wait()
    for b in range(8):
        asel[b * 32:(b + 1) * 32, :] = downv[owner_ref[b]]
        ub = 2.0 * ubf[b // 4, :, (b % 4) * 128:(b % 4 + 1) * 128].astype(F32)
        parts = []
        if b > 0:
            parts.append(jnp.zeros((b * 32, 128), F32))
        parts.append(ub)
        if b < 7:
            parts.append(jnp.zeros(((7 - b) * 32, 128), F32))
        ubd[b * 128:(b + 1) * 128, :] = jnp.concatenate(parts, axis=0).T.astype(BF)

    g_r1.wait_recv()
    g_l1.wait_recv()
    g_o = [gsend(6, 4, first, zdev(1, 0)), gsend(2, 4, last, zdev(3, 0))]

    def near_send(row_a, row_b, size):
        sent = []
        for d in (1, 3):
            for rel in (0, 1):
                slot = (4 - d) * 2 + rel
                at = row_a if slot < 5 else row_b
                dst_t = ((z + d) % 4) * 2 + (c + rel) % 2
                sent.append(
                    rcopy(
                        w_hbm.at[:, pl.ds(dst_t * 1024 + at, size), :],
                        wf.at[slot, :, pl.ds(at, size), :],
                        zdev(d, rel),
                    )
                )
        return sent

    w3 = []
    for i in (0, 3, 1):
        w3.append(
            near_send((((y + i) % 4) * 4 + xo) * 64, (((x + i) % 4) * 4 + yo) * 64, 64)
        )
    w3.append(near_send(yo * 256, xo * 256, 256))

    def product(slots, tile):
        start = pl.multiple_of(tile * 256, 256)
        pairs = [(s, ch) for s in slots for ch in range(2)]
        lhs = jnp.concatenate([gf[s, ch] for s, ch in pairs], axis=1)
        rhs = jnp.concatenate([wf[s, ch, pl.ds(start, 256), :] for s, ch in pairs], axis=1)
        return lax.dot_general(lhs, rhs, NT, preferred_element_type=F32)

    l_w.wait()
    w_s.wait_recv()
    g_s[0].wait_recv()

    def own_pass(i, carry):
        cols = pl.ds(pl.multiple_of(i * 256, 256), 256)
        acc[i] = product((0, 1), i) + jnp.dot(
            ubd[...], asel[:, cols], preferred_element_type=F32
        )
        return carry

    lax.fori_loop(0, 4, own_pass, 0)

    for cp in ag_1:
        cp.wait_recv()
    a_o1 = rcopy(row(aga, 384, 64, low), row(aga, 256, 64, low), xdev(1))
    a_o2 = rcopy(row(aga, 192, 64, low), row(aga, 320, 64, low), xdev(3))
    b_o1 = rcopy(row(agb, 384, 64, low), row(agb, 256, 64, low), ydev(1))
    b_o2 = rcopy(row(agb, 192, 64, low), row(agb, 320, 64, low), ydev(3))
    w2a += wsend(half_a, (y * 4 + xl) * 64, 64, ys)
    w2b += wsend(half_b, (x * 4 + yd) * 64, 64, xs)
    w2a += wsend(half_a, (y * 4 + xr) * 64, 64, ys)
    w2b += wsend(half_b, (x * 4 + yu) * 64, 64, xs)
    for cp in w1o:
        cp.wait_recv()
    w2a += wsend(far_a, (y * 4 + xo) * 64, 64, ys)
    w2b += wsend(far_b, (x * 4 + yo) * 64, 64, xs)
    g_r2.wait_recv()
    g_l2.wait_recv()
    g_s.append(rcopy(gf.at[6], gf.at[7], sib))
    g_s.append(rcopy(gf.at[2], gf.at[3], sib))

    def gathered(e, ag, k, n=1):
        return jnp.dot(e[k * 128:(k + n) * 128, :], ag[...], preferred_element_type=F32)

    rings = ((a_o1, a_o2, ea, aga, snd_a, r1_a, r2_a, own_a, dns_a, ydev),
             (b_o1, b_o2, eb, agb, snd_b, r1_b, r2_b, own_b, dns_b, xdev))
    steps = []
    for cp in ag_2:
        cp.wait_recv()
    for o1, o2, e, ag, snd, r1, r2, own, dns, dev in rings:
        o1.wait_recv()
        o2.wait_recv()
        snd[256:384, :] = gathered(e, ag, 2).astype(BF)
        s1 = rcopy(row(snd, 256, 64), row(r1, 0, 64), dev(1))
        s2 = rcopy(row(snd, 320, 64), row(r1, 64, 64), dev(3))
        steps.append([s1, s2])
    for step, (o1, o2, e, ag, snd, r1, r2, own, dns, dev) in zip(steps, rings):
        dn = gathered(e, ag, 3)
        snd[384:448, :] = dn[0:64].astype(BF)
        dns[64:128, :] = dn[64:128]
        up = gathered(e, ag, 0, 2)
        own[...] = up[0:128]
        snd[192:256, :] = up[192:256].astype(BF)
        dns[0:64, :] = up[128:192]
        step.append(rcopy(row(snd, 192, 64), row(r2, 64, 64), dev(1)))
        step.append(rcopy(row(snd, 384, 64), row(r2, 128, 64), dev(3)))

    for cp in g_o:
        cp.wait_recv()
    g_s.append(rcopy(gf.at[4], gf.at[5], sib))
    group_a, group_b = (2, 3, 4), (5, 6, 7)

    def near_pass(i, carry):
        ta, tb = (y + i) % 4, (x + i) % 4
        acc[ta] += product(group_a, ta)
        acc[tb] += product(group_b, tb)
        return carry

    for cp in w2a + w2b:
        cp.wait_recv()
    w2o = wsend(far_a, yd * 256, 128, ys[:1]) + wsend(far_a, yu * 256 + 128, 128, ys[1:])
    w2o += wsend(far_b, xl * 256, 128, xs[:1]) + wsend(far_b, xr * 256 + 128, 128, xs[1:])

    for step, (o1, o2, e, ag, snd, r1, r2, own, dns, dev) in zip(steps, rings):
        s1, s2, s3, s4 = step
        s1.wait_recv()
        snd[128:192, :] = (dns[0:64, :] + r1[0:64, :].astype(F32)).astype(BF)
        s5 = rcopy(row(snd, 128, 64), row(r2, 0, 64), dev(1))
        s2.wait_recv()
        snd[448:512, :] = (dns[64:128, :] + r1[64:128, :].astype(F32)).astype(BF)
        s6 = rcopy(row(snd, 448, 64), row(r2, 192, 64), dev(3))
        step += [s5, s6]

    for cp in g_s[1:] + w3[0]:
        cp.wait_recv()
    near_pass(0, 0)
    for cp in w3[1] + w3[2]:
        cp.wait_recv()

    def side_pass(i, carry):
        return near_pass(1 + 2 * i, carry)

    lax.fori_loop(0, 2, side_pass, 0)

    late = [cp for step in steps for cp in step[4:]]
    for cp in pending:
        if all(cp is not other for other in late):
            cp.wait_send()
    for cp in w3[3] + w2o:
        cp.wait_recv()
    near_pass(2, 0)
    for i in range(4):
        hg_out[:, i * 256:(i + 1) * 256] = acc[i].astype(BF)

    for ch, (step, (o1, o2, e, ag, snd, r1, r2, own, dns, dev)) in enumerate(zip(steps, rings)):
        for cp in step[2:]:
            cp.wait_recv()
        tot = 2.0 * (own[...] + r2[0:128, :].astype(F32) + r2[128:256, :].astype(F32))
        for q in range(8):
            ga_out[q, ch * 16:(ch + 1) * 16, :] = tot[q * 16:(q + 1) * 16, 0:1024]
            gb_out[q, ch] = tot[q * 16:(q + 1) * 16, 1024:1152]
    for cp in late:
        cp.wait_send()


def store_kernel(hg, ga, gb, hg_hbm, ga_hbm, gb_hbm, sems):
    parts = [(hg, hg_hbm, 256 * i, 256) for i in range(4)]
    parts += [(ga, ga_hbm, 4 * i, 4) for i in range(2)] + [(gb, gb_hbm, 0, 8)]
    copies = [
        pltpu.make_async_copy(src.at[pl.ds(at, size)], dst.at[pl.ds(at, size)], sems.at[k])
        for k, (src, dst, at, size) in enumerate(parts)
    ]
    for cp in copies:
        cp.start()
    for cp in copies:
        cp.wait()


def per_device(
    hidden_input,
    key_value_gradient,
    key_value_weight,
    down_adapters,
    up_adapters,
    adapter_inner_saved,
    block_owner_tenant,
    live_block_counts,
    tenant_position,
):
    hbm = pl.BlockSpec(memory_space=pltpu.HBM)
    smem = pl.BlockSpec(memory_space=pltpu.SMEM)
    v = pltpu.VMEM
    vmem = pl.BlockSpec(memory_space=pltpu.VMEM)
    vs = (pltpu.VMEM((1024, 1024), BF), pltpu.VMEM((8, 32, 1024), F32), pltpu.VMEM((8, 2, 16, 128), F32))
    shapes = (
        jax.ShapeDtypeStruct((1024, 1024), BF),
        jax.ShapeDtypeStruct((8, 32, 1024), F32),
        jax.ShapeDtypeStruct((8, 2, 16, 128), F32),
    )
    outs = pl.pallas_call(
        comm_kernel,
        out_shape=vs,
        in_specs=[hbm] * 6 + [smem] * 3,
        out_specs=(vmem, vmem, vmem),
        scratch_shapes=[
            v((8, 2, 1024, 128), BF),
            v((8, 2, 1024, 128), BF),
            v((1024, 1024), BF),
            v((128, 32, 1024), BF),
            v((128, 32, 128), BF),
            v((32, 1024), BF),
            v((2, 1024, 128), BF),
            v((2, 32, 512), F32),
            v((32, 512), F32),
            v((4, 32, 512), BF),
            v((2, 32, 512), BF),
            v((1024, 256), BF),
            v((256, 1024), BF),
            v((4, 8, 128), jnp.int32),
            v((4, 8, 128), jnp.int32),
            v((512, 512), BF),
            v((512, 512), BF),
            v((512, 1152), BF),
            v((512, 1152), BF),
            v((512, 1152), BF),
            v((512, 1152), BF),
            v((128, 1152), BF),
            v((128, 1152), BF),
            v((256, 1152), BF),
            v((256, 1152), BF),
            v((128, 1152), F32),
            v((128, 1152), F32),
            v((128, 1152), F32),
            v((128, 1152), F32),
            v((4, 1024, 256), F32),
            pltpu.SemaphoreType.DMA((N_REMOTE,)),
            pltpu.SemaphoreType.DMA((N_REMOTE,)),
            pltpu.SemaphoreType.DMA((N_LOCAL,)),
        ],
        compiler_params=pltpu.CompilerParams(
            collective_id=0, has_side_effects=True, vmem_limit_bytes=54 * 1024 * 1024
        ),
        name="projection_backward",
    )(
        hidden_input, key_value_gradient, key_value_weight, down_adapters,
        up_adapters.reshape(128, 32, 128), adapter_inner_saved,
        block_owner_tenant, live_block_counts, tenant_position,
    )
    return pl.pallas_call(
        store_kernel,
        out_shape=shapes,
        in_specs=[pl.BlockSpec(memory_space=pl.ANY)] * 3,
        out_specs=(hbm, hbm, hbm),
        scratch_shapes=[pltpu.SemaphoreType.DMA((7,))],
        name="store_outputs",
    )(*[pltpu.with_memory_space_constraint(o, pltpu.VMEM) for o in outs])


def solution(mesh):
    return jax.shard_map(
        per_device,
        mesh=mesh,
        in_specs=(
            P("dp", None),
            P(None, "dp", "tensor"),
            P(None, None, "tensor"),
            P(None, None, "tensor"),
            P(None, None, None, "tensor"),
            P(None, "dp"),
            P("dp"),
            P("dp"),
            P(),
        ),
        out_specs=(P("dp", "tensor"), P("dp", None, "tensor"), P("dp", None, None, "tensor")),
        check_vma=False,
    )
```

```python
import jax
import jax.numpy as jnp
from jax import lax
from jax.experimental import pallas as pl
from jax.experimental.pallas import tpu as pltpu
from jax.sharding import PartitionSpec as P

MESH = pl.DeviceIdType.MESH
BF = jnp.bfloat16
F32 = jnp.float32
NT = (((1,), (1,)), ((), ()))
N_REMOTE = 120
N_LOCAL = 6


def comm_kernel(
    x_hbm, kvg_hbm, w_hbm, down_hbm, up_hbm, inner_hbm, owner_ref, live_ref, tp_ref,
    hg_out, ga_out, gb_out,
    gf, wf, xv, downv, upv, innerv, kvgv,
    upart, urecv, uz, ubf, ubd, asel,
    meta_a, meta_b, ea, eb, aga, agb,
    snd_a, snd_b, r1_a, r1_b, r2_a, r2_b, own_a, own_b, dns_a, dns_b,
    acc,
    ss, rs, ls,
):
    dp = lax.axis_index("dp")
    t = lax.axis_index("tensor")
    y, x = dp // 4, dp % 4
    z, c = t // 2, t % 2

    def xdev(d):
        return (y * 4 + (x + d) % 4, t)

    def ydev(d):
        return (((y + d) % 4) * 4 + x, t)

    def zdev(d, rel):
        return (dp, ((z + d) % 4) * 2 + (c + rel) % 2)

    sib = zdev(0, 1)
    count = [0, 0]
    pending = []

    def rcopy(src, dst, dev):
        k = count[0]
        count[0] += 1
        cp = pltpu.make_async_remote_copy(
            src_ref=src, dst_ref=dst, send_sem=ss.at[k], recv_sem=rs.at[k],
            device_id=dev, device_id_type=MESH,
        )
        cp.start()
        pending.append(cp)
        return cp

    def lcopy(src, dst):
        k = count[1]
        count[1] += 1
        cp = pltpu.make_async_copy(src, dst, ls.at[k])
        cp.start()
        return cp

    peers = [sib]
    peers += [zdev(d, rel) for d in (1, 2, 3) for rel in (0, 1)]
    peers += [xdev(d) for d in (1, 2, 3)] + [ydev(d) for d in (1, 2, 3)]
    barrier = pltpu.get_barrier_semaphore()
    for dev in peers:
        pl.semaphore_signal(barrier, inc=1, device_id=dev, device_id_type=MESH)

    l_kvg = lcopy(kvg_hbm, kvgv)
    l_up = lcopy(up_hbm, upv)
    l_inner = lcopy(inner_hbm, innerv)

    lane = lax.broadcasted_iota(jnp.int32, (8, 128), 1)
    pos = jnp.zeros((8, 128), jnp.int32)
    for b in range(8):
        pos = jnp.where((lane >> 4) == b, tp_ref[owner_ref[b]], pos)
    meta_a[0] = pos
    meta_b[0] = pos

    pl.semaphore_wait(barrier, len(peers))

    qa = y * 4 + x
    qb = x * 4 + y
    w1 = []
    for d, rel in ((1, 0), (3, 0), (1, 1), (3, 1), (2, 0), (2, 1)):
        slot = (4 - d) * 2 + rel
        q = qa if slot < 5 else qb
        dst_t = ((z + d) % 4) * 2 + (c + rel) % 2
        w1.append(
            rcopy(
                w_hbm.at[:, pl.ds(dst_t * 1024 + q * 64, 64), :],
                wf.at[slot, :, pl.ds(q * 64, 64), :],
                zdev(d, rel),
            )
        )
    m1 = []
    for d in (1, 2, 3):
        m1.append(rcopy(meta_a.at[0], meta_a.at[4 - d], xdev(d)))
        m1.append(rcopy(meta_b.at[0], meta_b.at[4 - d], ydev(d)))
    l_x = lcopy(x_hbm.at[:, pl.ds(t * 1024, 1024)], xv)

    l_kvg.wait()
    l_up.wait()
    live = live_ref[0]
    off = jnp.zeros((16, 128), BF)
    for b in range(8):
        rows = pl.ds(b * 128, 128)
        upb = upv[owner_ref[b]]
        up2 = jnp.concatenate(
            [jnp.concatenate([upb[0:16], off], axis=1), jnp.concatenate([off, upb[16:32]], axis=1)],
            axis=0,
        )
        g2 = []
        for ch in range(2):
            g = kvgv[ch, rows, :]
            g2.append(jnp.where(b < live, g, jnp.zeros_like(g)))
            gf[0, ch, rows, :] = g2[ch]
        upart[b // 4, :, (b % 4) * 128:(b % 4 + 1) * 128] = lax.dot_general(
            up2, jnp.concatenate(g2, axis=1), NT, preferred_element_type=F32
        )
    u1 = rcopy(upart.at[1 - c], urecv, sib)
    l_inner.wait()
    for b in range(8):
        rows = pl.ds(b * 128, 128)
        for ch, ag in ((0, aga), (1, agb)):
            ag[b * 16:(b + 1) * 16, 1024:1152] = jnp.dot(
                innerv[ch * 16:(ch + 1) * 16, b * 128:(b + 1) * 128], gf[0, ch, rows, :],
                preferred_element_type=F32,
            ).astype(BF)

    def row(ref, start, size, cols=slice(None)):
        return ref.at[pl.ds(start, size), cols]

    low, high = pl.ds(0, 1024), pl.ds(1024, 128)
    bg = []
    for ag, dev in ((aga, xdev), (agb, ydev)):
        bg.append(rcopy(row(ag, 0, 128, high), row(ag, 384, 128, high), dev(1)))
        bg.append(rcopy(row(ag, 0, 128, high), row(ag, 128, 128, high), dev(3)))

    def wsend(slots, row, size, devs):
        part = wf.at[slots, :, pl.ds(row, size), :]
        return [rcopy(part, part, dev) for dev in devs]

    xs, ys = (xdev(1), xdev(3)), (ydev(1), ydev(3))
    half_a, half_b = pl.ds(2, 3), pl.ds(5, 3)
    wa1, wb1, w2a, w2b = [], [], [], []

    def start_rings(slots_a, slots_b):
        wa1.extend(wsend(slots_a, qa * 64, 64, xs))
        wb1.extend(wsend(slots_b, qb * 64, 64, ys))
        w2a.extend(wsend(slots_a, qa * 64, 64, ys))
        w2b.extend(wsend(slots_b, qb * 64, 64, xs))

    u1.wait_recv()
    uz[0] = (upart[c] + urecv[...]).astype(BF)
    u2 = [rcopy(uz.at[0], uz.at[4 - d], zdev(d, 0)) for d in (1, 3, 2)]
    for cp in w1[:2]:
        cp.wait_recv()
    start_rings(pl.ds(2, 1), pl.ds(6, 1))
    first, last = pl.ds(0, 512), pl.ds(512, 512)

    def gsend(slot, dst, part, dev):
        return rcopy(gf.at[slot, :, part, :], gf.at[dst, :, part, :], dev)

    g_r1 = gsend(0, 6, first, zdev(1, 0))
    g_l1 = gsend(0, 2, last, zdev(3, 0))
    g_r2 = gsend(0, 6, last, zdev(1, 0))
    g_l2 = gsend(0, 2, first, zdev(3, 0))
    for cp in w1[2:4]:
        cp.wait_recv()
    start_rings(pl.ds(3, 1), pl.ds(7, 1))
    for cp in w1[4:]:
        cp.wait_recv()
    start_rings(pl.ds(4, 1), pl.ds(5, 1))
    l_w = lcopy(w_hbm.at[:, pl.ds(t * 1024, 1024), :], wf.at[0])
    l_down = lcopy(down_hbm, downv)

    for cp in u2:
        cp.wait_recv()
    ubf[c] = (
        uz[0].astype(F32) + uz[1].astype(F32) + uz[2].astype(F32) + uz[3].astype(F32)
    ).astype(BF)
    u3 = rcopy(ubf.at[c], ubf.at[c], sib)

    l_x.wait()
    u3.wait_recv()
    for b in range(8):
        ub = ubf[b // 4, :, (b % 4) * 128:(b % 4 + 1) * 128]
        term = jnp.dot(ub, xv[b * 128:(b + 1) * 128, :], preferred_element_type=F32).astype(BF)
        aga[b * 16:(b + 1) * 16, 0:1024] = term[0:16]
        agb[b * 16:(b + 1) * 16, 0:1024] = term[16:32]

    ag_1, ag_2 = [], []
    for ag, dev in ((aga, xdev), (agb, ydev)):
        ag_1.append(rcopy(row(ag, 0, 64, low), row(ag, 384, 64, low), dev(1)))
        ag_1.append(rcopy(row(ag, 64, 64, low), row(ag, 192, 64, low), dev(3)))
    for ag, dev in ((aga, xdev), (agb, ydev)):
        ag_2.append(rcopy(row(ag, 64, 64, low), row(ag, 448, 64, low), dev(1)))
        ag_2.append(rcopy(row(ag, 0, 64, low), row(ag, 128, 64, low), dev(3)))
    for cp in bg:
        cp.wait_recv()
    for ag, dev in ((aga, xdev), (agb, ydev)):
        ag_2.append(rcopy(row(ag, 384, 64, high), row(ag, 256, 64, high), dev(1)))
        ag_2.append(rcopy(row(ag, 192, 64, high), row(ag, 320, 64, high), dev(3)))
    g_s = [rcopy(gf.at[0], gf.at[1], sib)]
    w_s = rcopy(w_hbm.at[:, pl.ds(sib[1] * 1024, 1024), :], wf.at[1], sib)

    xl, xr, xo = (x + 3) % 4, (x + 1) % 4, (x + 2) % 4
    yd, yu, yo = (y + 3) % 4, (y + 1) % 4, (y + 2) % 4
    for cp in wa1 + wb1:
        cp.wait_recv()
    far_a, far_b = pl.ds(4, 1), pl.ds(5, 1)
    w1o = wsend(far_a, (y * 4 + xl) * 64, 32, xs[:1])
    w1o += wsend(far_a, (y * 4 + xr) * 64 + 32, 32, xs[1:])
    w1o += wsend(far_b, (x * 4 + yd) * 64, 32, ys[:1])
    w1o += wsend(far_b, (x * 4 + yu) * 64 + 32, 32, ys[1:])

    for cp in m1:
        cp.wait_recv()
    out_row = lax.broadcasted_iota(jnp.int32, (512, 128), 0)
    lane1 = lax.broadcasted_iota(jnp.int32, (1, 128), 1)
    for s in range(4):
        for meta, e, ring, other, mine in (
            (meta_a, ea, 0, 2, (x, y)), (meta_b, eb, 2, 0, (y, x)),
        ):
            p = meta[s, 0:1, :]
            owner = p >> 3
            valid = ((owner >> ring) & 3) == mine[0]
            dest = (((owner >> other) & 3) - mine[1]) & 3
            target = jnp.where(valid, dest * 128 + (p & 7) * 16 + (lane1 & 15), -1)
            e[:, s * 128:(s + 1) * 128] = (out_row == target).astype(F32).astype(BF)

    l_down.wait()
    for b in range(8):
        asel[b * 32:(b + 1) * 32, :] = downv[owner_ref[b]]
        ub = 2.0 * ubf[b // 4, :, (b % 4) * 128:(b % 4 + 1) * 128].astype(F32)
        parts = []
        if b > 0:
            parts.append(jnp.zeros((b * 32, 128), F32))
        parts.append(ub)
        if b < 7:
            parts.append(jnp.zeros(((7 - b) * 32, 128), F32))
        ubd[b * 128:(b + 1) * 128, :] = jnp.concatenate(parts, axis=0).T.astype(BF)

    g_r1.wait_recv()
    g_l1.wait_recv()
    g_o = [gsend(6, 4, first, zdev(1, 0)), gsend(2, 4, last, zdev(3, 0))]

    def near_send(row_a, row_b, size):
        sent = []
        for d in (1, 3):
            for rel in (0, 1):
                slot = (4 - d) * 2 + rel
                at = row_a if slot < 5 else row_b
                dst_t = ((z + d) % 4) * 2 + (c + rel) % 2
                sent.append(
                    rcopy(
                        w_hbm.at[:, pl.ds(dst_t * 1024 + at, size), :],
                        wf.at[slot, :, pl.ds(at, size), :],
                        zdev(d, rel),
                    )
                )
        return sent

    w3 = []
    for i in (0, 3, 1):
        w3.append(
            near_send((((y + i) % 4) * 4 + xo) * 64, (((x + i) % 4) * 4 + yo) * 64, 64)
        )
    w3.append(near_send(yo * 256, xo * 256, 256))

    def product(slots, tile):
        start = pl.multiple_of(tile * 256, 256)
        pairs = [(s, ch) for s in slots for ch in range(2)]
        lhs = jnp.concatenate([gf[s, ch] for s, ch in pairs], axis=1)
        rhs = jnp.concatenate([wf[s, ch, pl.ds(start, 256), :] for s, ch in pairs], axis=1)
        return lax.dot_general(lhs, rhs, NT, preferred_element_type=F32)

    l_w.wait()
    w_s.wait_recv()
    g_s[0].wait_recv()

    def own_pass(i, carry):
        cols = pl.ds(pl.multiple_of(i * 256, 256), 256)
        acc[i] = product((0, 1), i) + jnp.dot(
            ubd[...], asel[:, cols], preferred_element_type=F32
        )
        return carry

    lax.fori_loop(0, 4, own_pass, 0)

    for cp in ag_1:
        cp.wait_recv()
    a_o1 = rcopy(row(aga, 384, 64, low), row(aga, 256, 64, low), xdev(1))
    a_o2 = rcopy(row(aga, 192, 64, low), row(aga, 320, 64, low), xdev(3))
    b_o1 = rcopy(row(agb, 384, 64, low), row(agb, 256, 64, low), ydev(1))
    b_o2 = rcopy(row(agb, 192, 64, low), row(agb, 320, 64, low), ydev(3))
    w2a += wsend(half_a, (y * 4 + xl) * 64, 64, ys)
    w2b += wsend(half_b, (x * 4 + yd) * 64, 64, xs)
    w2a += wsend(half_a, (y * 4 + xr) * 64, 64, ys)
    w2b += wsend(half_b, (x * 4 + yu) * 64, 64, xs)
    for cp in w1o:
        cp.wait_recv()
    w2a += wsend(far_a, (y * 4 + xo) * 64, 64, ys)
    w2b += wsend(far_b, (x * 4 + yo) * 64, 64, xs)
    g_r2.wait_recv()
    g_l2.wait_recv()
    g_s.append(rcopy(gf.at[6], gf.at[7], sib))
    g_s.append(rcopy(gf.at[2], gf.at[3], sib))

    def gathered(e, ag, k, n=1):
        return jnp.dot(e[k * 128:(k + n) * 128, :], ag[...], preferred_element_type=F32)

    rings = ((a_o1, a_o2, ea, aga, snd_a, r1_a, r2_a, own_a, dns_a, ydev),
             (b_o1, b_o2, eb, agb, snd_b, r1_b, r2_b, own_b, dns_b, xdev))
    steps = []
    for cp in ag_2:
        cp.wait_recv()
    for o1, o2, e, ag, snd, r1, r2, own, dns, dev in rings:
        o1.wait_recv()
        o2.wait_recv()
        snd[256:384, :] = gathered(e, ag, 2).astype(BF)
        s1 = rcopy(row(snd, 256, 64), row(r1, 0, 64), dev(1))
        s2 = rcopy(row(snd, 320, 64), row(r1, 64, 64), dev(3))
        steps.append([s1, s2])
    for step, (o1, o2, e, ag, snd, r1, r2, own, dns, dev) in zip(steps, rings):
        dn = gathered(e, ag, 3)
        snd[384:448, :] = dn[0:64].astype(BF)
        dns[64:128, :] = dn[64:128]
        up = gathered(e, ag, 0, 2)
        own[...] = up[0:128]
        snd[192:256, :] = up[192:256].astype(BF)
        dns[0:64, :] = up[128:192]
        step.append(rcopy(row(snd, 192, 64), row(r2, 64, 64), dev(1)))
        step.append(rcopy(row(snd, 384, 64), row(r2, 128, 64), dev(3)))

    for cp in g_o:
        cp.wait_recv()
    g_s.append(rcopy(gf.at[4], gf.at[5], sib))
    group_a, group_b = (2, 3, 4), (5, 6, 7)

    def near_pass(i, carry):
        ta, tb = (y + i) % 4, (x + i) % 4
        acc[ta] += product(group_a, ta)
        acc[tb] += product(group_b, tb)
        return carry

    for cp in w2a + w2b:
        cp.wait_recv()
    w2o = wsend(far_a, yd * 256, 128, ys[:1]) + wsend(far_a, yu * 256 + 128, 128, ys[1:])
    w2o += wsend(far_b, xl * 256, 128, xs[:1]) + wsend(far_b, xr * 256 + 128, 128, xs[1:])

    for step, (o1, o2, e, ag, snd, r1, r2, own, dns, dev) in zip(steps, rings):
        s1, s2, s3, s4 = step
        s1.wait_recv()
        snd[128:192, :] = (dns[0:64, :] + r1[0:64, :].astype(F32)).astype(BF)
        s5 = rcopy(row(snd, 128, 64), row(r2, 0, 64), dev(1))
        s2.wait_recv()
        snd[448:512, :] = (dns[64:128, :] + r1[64:128, :].astype(F32)).astype(BF)
        s6 = rcopy(row(snd, 448, 64), row(r2, 192, 64), dev(3))
        step += [s5, s6]

    for cp in g_s[1:] + w3[0]:
        cp.wait_recv()
    near_pass(0, 0)
    for cp in w3[1] + w3[2]:
        cp.wait_recv()

    def side_pass(i, carry):
        return near_pass(1 + 2 * i, carry)

    lax.fori_loop(0, 2, side_pass, 0)

    late = [cp for step in steps for cp in step[4:]]
    for cp in pending:
        if all(cp is not other for other in late):
            cp.wait_send()
    for cp in w3[3] + w2o:
        cp.wait_recv()
    near_pass(2, 0)
    for i in range(4):
        hg_out[:, i * 256:(i + 1) * 256] = acc[i].astype(BF)

    for ch, (step, (o1, o2, e, ag, snd, r1, r2, own, dns, dev)) in enumerate(zip(steps, rings)):
        for cp in step[2:]:
            cp.wait_recv()
        tot = 2.0 * (own[...] + r2[0:128, :].astype(F32) + r2[128:256, :].astype(F32))
        for q in range(8):
            ga_out[q, ch * 16:(ch + 1) * 16, :] = tot[q * 16:(q + 1) * 16, 0:1024]
            gb_out[q, ch] = tot[q * 16:(q + 1) * 16, 1024:1152]
    for cp in late:
        cp.wait_send()


def store_kernel(hg, ga, gb, hg_hbm, ga_hbm, gb_hbm, sems):
    parts = [(hg, hg_hbm, 256 * i, 256) for i in range(4)]
    parts += [(ga, ga_hbm, 4 * i, 4) for i in range(2)] + [(gb, gb_hbm, 0, 8)]
    copies = [
        pltpu.make_async_copy(src.at[pl.ds(at, size)], dst.at[pl.ds(at, size)], sems.at[k])
        for k, (src, dst, at, size) in enumerate(parts)
    ]
    for cp in copies:
        cp.start()
    for cp in copies:
        cp.wait()


def per_device(
    hidden_input,
    key_value_gradient,
    key_value_weight,
    down_adapters,
    up_adapters,
    adapter_inner_saved,
    block_owner_tenant,
    live_block_counts,
    tenant_position,
):
    hbm = pl.BlockSpec(memory_space=pltpu.HBM)
    smem = pl.BlockSpec(memory_space=pltpu.SMEM)
    v = pltpu.VMEM
    vmem = pl.BlockSpec(memory_space=pltpu.VMEM)
    vs = (pltpu.VMEM((1024, 1024), BF), pltpu.VMEM((8, 32, 1024), F32), pltpu.VMEM((8, 2, 16, 128), F32))
    shapes = (
        jax.ShapeDtypeStruct((1024, 1024), BF),
        jax.ShapeDtypeStruct((8, 32, 1024), F32),
        jax.ShapeDtypeStruct((8, 2, 16, 128), F32),
    )
    outs = pl.pallas_call(
        comm_kernel,
        out_shape=vs,
        in_specs=[hbm] * 6 + [smem] * 3,
        out_specs=(vmem, vmem, vmem),
        scratch_shapes=[
            v((8, 2, 1024, 128), BF),
            v((8, 2, 1024, 128), BF),
            v((1024, 1024), BF),
            v((128, 32, 1024), BF),
            v((128, 32, 128), BF),
            v((32, 1024), BF),
            v((2, 1024, 128), BF),
            v((2, 32, 512), F32),
            v((32, 512), F32),
            v((4, 32, 512), BF),
            v((2, 32, 512), BF),
            v((1024, 256), BF),
            v((256, 1024), BF),
            v((4, 8, 128), jnp.int32),
            v((4, 8, 128), jnp.int32),
            v((512, 512), BF),
            v((512, 512), BF),
            v((512, 1152), BF),
            v((512, 1152), BF),
            v((512, 1152), BF),
            v((512, 1152), BF),
            v((128, 1152), BF),
            v((128, 1152), BF),
            v((256, 1152), BF),
            v((256, 1152), BF),
            v((128, 1152), F32),
            v((128, 1152), F32),
            v((128, 1152), F32),
            v((128, 1152), F32),
            v((4, 1024, 256), F32),
            pltpu.SemaphoreType.DMA((N_REMOTE,)),
            pltpu.SemaphoreType.DMA((N_REMOTE,)),
            pltpu.SemaphoreType.DMA((N_LOCAL,)),
        ],
        compiler_params=pltpu.CompilerParams(
            collective_id=0, has_side_effects=True, vmem_limit_bytes=54 * 1024 * 1024
        ),
        name="projection_backward",
    )(
        hidden_input, key_value_gradient, key_value_weight, down_adapters,
        up_adapters.reshape(128, 32, 128), adapter_inner_saved,
        block_owner_tenant, live_block_counts, tenant_position,
    )
    return pl.pallas_call(
        store_kernel,
        out_shape=shapes,
        in_specs=[pl.BlockSpec(memory_space=pl.ANY)] * 3,
        out_specs=(hbm, hbm, hbm),
        scratch_shapes=[pltpu.SemaphoreType.DMA((7,))],
        name="store_outputs",
    )(*[pltpu.with_memory_space_constraint(o, pltpu.VMEM) for o in outs])


def solution(mesh):
    return jax.shard_map(
        per_device,
        mesh=mesh,
        in_specs=(
            P("dp", None),
            P(None, "dp", "tensor"),
            P(None, None, "tensor"),
            P(None, None, "tensor"),
            P(None, None, None, "tensor"),
            P(None, "dp"),
            P("dp"),
            P("dp"),
            P(),
        ),
        out_specs=(P("dp", "tensor"), P("dp", None, "tensor"), P("dp", None, None, "tensor")),
        check_vma=False,
    )
```
